128 devices in a mesh: section: 2 (over core), dp: 64 (over z, y, x).
Axes of the slice: x: 4, y: 4, z: 4, core: 2. Of those that a mesh axis runs over, the one named last changes fastest.
Arguments:
- activations: bfloat16 [128, 6, 192, 2560], P(('section', 'dp')), parts along dimension 0, may hold values from -16 to 16
- cotangents: bfloat16 [128, 6, 192, 2560], P(('section', 'dp')), parts along dimension 0, may hold values from -1.5 to 1.5
- failed: int32 [1], replicated, may hold values from 0 to 63
- counts: int32 [64], P('dp'), may hold values from 1 to 6, as said below
- order: int32 [64, 6], P('dp'), may hold values from 0 to 5, each once within a row
Outputs:
- gradient: float32 [5120, 2560], P(('section', 'dp')), parts along dimension 0
The draws below stay inside these ranges and needn't reach their ends.
There are 2 independent parts, one for each index of `section`. The reference program is written for one: setup_inputs(seed, part) draws one part's arguments, and reference() takes and returns one part's arrays. A program takes and returns all parts, laid end to end along the dimension named above; an argument that names none is the same for every part. Nothing has to cross between parts.
Inputs may be any that keep to these rules, and one draw needn't show every extreme that they name: `counts`: each replica reports 1 to 6 micro-batches; some replica reports exactly 6.
All inputs are finite; a program needn't handle non-finite values.
Results may differ from the reference program's by a relative error of at most 0.0003.
Values sent between devices are 32-bit elements; how exact they have to be, the bound alone decides.
No kernel may reach another device: no remote copies, remote signals or barrier semaphores. Data moves between devices by JAX's collectives and lax.ppermute only.
A program may use at most 320 MiB of HBM per device.

```python
import jax
import jax.numpy as jnp

IN = 2560
OUT = 2560
M = 192
SLOTS = 6
DP = 64


def draw_counts(key, part):
    reported = jax.random.randint(jax.random.fold_in(key, 11), (DP,), 1, SLOTS + 1)
    busiest = jax.random.randint(jax.random.fold_in(key, 12), (), 0, DP)
    replica_group = jnp.arange(DP, dtype=jnp.int32)
    return jnp.where(replica_group == busiest, SLOTS, reported).astype(jnp.int32)


def strengthened(entries, key, source, target, parts, factor):
    owner, partner = [(jnp.arange(entries.shape[axis_at]) // (entries.shape[axis_at] // parts)).reshape([-1 if axis == axis_at else 1 for axis in range(entries.ndim)]) for axis_at in (source, target)]
    chosen = jax.random.permutation(key, parts)[partner]
    strong = (owner == chosen) | (owner == (partner + parts // 2) % parts)
    return jnp.where(strong, factor * entries, entries)


def steps_of(own_key, shape, pieces, smallest, high):
    def one(dim, shards_of):
        steps = jax.random.uniform(jax.random.fold_in(jax.random.fold_in(own_key, 6), dim), (shards_of,), jnp.float32, smallest / len(pieces), high / len(pieces))
        return jnp.repeat(jnp.exp(steps), shape[dim] // shards_of).reshape((-1,) + (1,) * (len(shape) - dim - 1))

    loudness = one(*pieces[0])
    for cut in pieces[1:]:
        loudness = loudness * one(*cut)
    return loudness


def noise(own_key, dims, deviation, most, cuts=(), held_as=jnp.bfloat16):
    array = jax.random.normal(own_key, dims, jnp.float32) * deviation
    if len(cuts) > 0:
        array = steps_of(own_key, dims, cuts, -0.22, 0.18) * array
    return jnp.clip(array, min=-most, max=most).astype(held_as)


def gaussian_with(rng, shape, width, bound, shards, heavy, held_as=jnp.bfloat16):
    array = width * jax.random.normal(rng, shape, jnp.float32)
    if shards:
        array = array * steps_of(rng, shape, shards, -0.22, 0.18)
    return jnp.clip(strengthened(array, jax.random.fold_in(rng, 3), *heavy), -bound, bound).astype(held_as)


def setup_inputs(seed: int = 0, part: int = 0) -> dict:
    seeds = jax.random.split(jax.random.key(seed), 6)
    part_keys = jax.random.split(jax.random.fold_in(seeds[5], part), 6)
    return {
        "activations": gaussian_with(part_keys[0], (DP, SLOTS, M, IN), 1.0, 16.0, ((0, 64),), (0, 3, 64, 4.0)),
        "cotangents": noise(part_keys[1], (DP, SLOTS, M, OUT), 0.25, 1.5, ((0, 64),)),
        "failed": jax.random.randint(seeds[2], (1,), 0, DP).astype(jnp.int32),
        "counts": draw_counts(jax.random.fold_in(seeds[5], 71), part),
        "order": jax.vmap(lambda own: jax.random.permutation(own, SLOTS))(jax.random.split(seeds[4], DP)).reshape((DP, SLOTS)).astype(jnp.int32),
    }


def reference(activations, cotangents, failed, counts, order):
    partial_gradient = jnp.zeros((IN, OUT), jnp.float32)
    for replica in range(DP):
        for position in range(SLOTS):
            selected_replica = order[replica, position]
            live = jnp.logical_and(position < counts[replica], replica != failed[0])
            weight_live = jnp.where(live, 1.0, 0.0).astype(jnp.bfloat16)
            act_rows = activations[replica, selected_replica]
            cot_rows = cotangents[replica, selected_replica] * weight_live
            partial_gradient = partial_gradient + jnp.dot(act_rows.T, cot_rows, preferred_element_type=jnp.float32)
    replica_group = jnp.arange(DP, dtype=jnp.int32)
    remaining_replica_total = jnp.sum(jnp.where(replica_group != failed[0], counts, 0)).astype(jnp.float32)
    return partial_gradient / remaining_replica_total
```

```python
import functools

import jax
import jax.numpy as jnp
from jax import lax
from jax.experimental import pallas as pl
from jax.experimental.pallas import tpu as pltpu
from jax.sharding import PartitionSpec as P

SLOTS, TOKENS, ROWS = 6, 192, 40
K = SLOTS * TOKENS
TILE = 16 * ROWS
STRIDE = {"x": 1, "y": 4, "z": 16}
COLOURS = ((0, 896, "xyz"), (896, 640, "yxz"), (1536, 1024, "zyx"))


def exchange(value, axis, turn):
    pairs = []
    for section in range(2):
        flip = 1 if section == turn else 3
        for d in range(64):
            p = d // STRIDE[axis] % 4
            pairs.append((section * 64 + d, section * 64 + d + ((p ^ flip) - p) * STRIDE[axis]))
    return lax.ppermute(value, ("section", "dp"), pairs)


def masked(place, cot_ref, cotm):
    for k in range(SLOTS):
        live = (place[12 + k] > 0).astype(jnp.float32)
        cotm[k * TOKENS:(k + 1) * TOKENS, :] = (cot_ref[0, k].astype(jnp.float32) * live).astype(jnp.bfloat16)


def z_first(place, act_ref, cot_ref, one_ref, two_ref, cotm, total):
    @pl.when(pl.program_id(0) == 0)
    def _():
        masked(place, cot_ref, cotm)
    total[...] = lax.dot_general(
        act_ref[...].reshape(K, TILE), cotm[...], (((0,), (0,)), ((), ())), preferred_element_type=jnp.float32)
    for sy in range(4):
        for sx in range(4):
            start = pl.multiple_of(place[4 + sy] * 160 + place[sx] * 40, 8)
            (two_ref if sx < 2 else one_ref)[0, sy, sx % 2] = total[pl.ds(start, ROWS), :]


def z_last(first, place, act_ref, cot_ref, send_ref, keep_ref, cotm, total):
    @pl.when(pl.program_id(0) == 0)
    def _():
        masked(place, cot_ref, cotm)
    total[...] = lax.dot_general(
        act_ref[...].reshape(K, TILE), cotm[...], (((0,), (0,)), ((), ())), preferred_element_type=jnp.float32)
    for sy in range(4):
        for sx in range(4):
            start = pl.multiple_of(place[4 + sy] * 160 + place[sx] * 40, 8)
            major, minor = (sx, sy) if first == "x" else (sy, sx)
            (keep_ref if major < 2 else send_ref)[major % 2, minor, 0] = total[pl.ds(start, ROWS), :]


def partials(colour, half, activations, cotangents, place):
    column, columns, axes = COLOURS[colour]
    if axes[0] == "z":
        kernel = z_first
        shape = (2, 4, 2, ROWS, columns)
        out = pl.BlockSpec((1, 4, 2, ROWS, columns), lambda g, s: (g, 0, 0, 0, 0))
    else:
        kernel = functools.partial(z_last, axes[0])
        shape = (2, 4, 2, ROWS, columns)
        out = pl.BlockSpec((2, 4, 1, ROWS, columns), lambda g, s: (0, 0, g, 0, 0))
    return pl.pallas_call(
        kernel,
        out_shape=[jax.ShapeDtypeStruct(shape, jnp.float32)] * 2,
        grid_spec=pltpu.PrefetchScalarGridSpec(
            num_scalar_prefetch=1,
            grid=(2,),
            in_specs=[
                pl.BlockSpec((1, SLOTS, TOKENS, TILE), lambda g, s: (0, 0, 0, s[8 + half + g])),
                pl.BlockSpec(tuple(map(pl.Element, (1, SLOTS, TOKENS, columns))), lambda g, s: (0, 0, 0, column)),
            ],
            out_specs=[out] * 2,
            scratch_shapes=[pltpu.VMEM((K, columns), jnp.bfloat16), pltpu.VMEM((TILE, columns), jnp.float32)],
        ),
        compiler_params=pltpu.CompilerParams(vmem_limit_bytes=40 << 20),
        cost_estimate=pl.CostEstimate(
            flops=2 * K * 2 * TILE * columns,
            bytes_accessed=K * 2 * TILE * 2 + K * columns * 2 + 2 * TILE * columns * 4,
            transcendentals=0,
        ),
    )(place, activations, cotangents)


def scattered(axes, halves):
    after_first = []
    for send, keep in halves:
        got = exchange(send, axes[0], 0)
        late = exchange(keep[1] + got[1], axes[0], 1)
        after_first.append((keep[0] + got[0]) + late)
    after_second = []
    for whole in after_first:
        got = exchange(whole[2:4], axes[1], 0)
        late = exchange(whole[1] + got[1], axes[1], 1)
        after_second.append((whole[0] + got[0]) + late)
    far, near = after_second
    got = exchange(far, axes[2], 0)
    late = exchange(near[1] + got[1], axes[2], 1)
    return (near[0] + got[0]) + late


def shards(activations, cotangents, failed, counts, order):
    section, me = lax.axis_index("section"), lax.axis_index("dp")
    alive = jnp.where(me == failed[0], 0, counts[0])
    live = jnp.zeros((SLOTS,), jnp.int32).at[order[0]].set((jnp.arange(SLOTS) < alive).astype(jnp.int32))
    flips = jnp.where(section == 0, jnp.array([0, 3, 1, 2]), jnp.array([0, 1, 3, 2])).astype(jnp.int32)
    place = jnp.concatenate([me % 4 ^ flips, me // 4 % 4 ^ flips, me // 16 ^ flips, live])
    total = lax.psum(alive.astype(jnp.float32), "dp")

    run = lambda colour, half: partials(colour, half, activations, cotangents, place)
    a_far = run(0, 2)
    b_far = run(1, 2)
    c_send = run(2, 2)
    a_near = run(0, 0)
    b_near = run(1, 0)
    c_keep = run(2, 0)
    a = scattered(COLOURS[0][2], (a_far, a_near))
    b = scattered(COLOURS[1][2], (b_far, b_near))
    c = scattered(COLOURS[2][2], ((c_send[0], c_keep[0]), (c_send[1], c_keep[1])))
    return jnp.concatenate([a, b, c], axis=1) / total


def solution(mesh):
    in_specs = (
        P(("section", "dp"), None, None, None),
        P(("section", "dp"), None, None, None),
        P(),
        P("dp"),
        P("dp", None),
    )
    out_specs = P(("section", "dp"), None)
    return jax.shard_map(shards, mesh=mesh, in_specs=in_specs, out_specs=out_specs, check_vma=False)
```

```python
import functools

import jax
import jax.numpy as jnp
from jax import lax
from jax.experimental import pallas as pl
from jax.experimental.pallas import tpu as pltpu
from jax.sharding import PartitionSpec as P

SLOTS, TOKENS, ROWS = 6, 192, 40
K = SLOTS * TOKENS
TILE = 16 * ROWS
STRIDE = {"x": 1, "y": 4, "z": 16}
COLOURS = ((0, 768, ("xyz", "xyz")), (768, 768, ("yxz", "yxz")), (1536, 1024, ("zyx", "zxy")))


def exchange(value, axes, turn):
    pairs = []
    for section in range(2):
        flip, stride = 1 if section == turn else 3, STRIDE[axes[section]]
        for d in range(64):
            p = d // stride % 4
            pairs.append((section * 64 + d, section * 64 + d + ((p ^ flip) - p) * stride))
    return lax.ppermute(value, ("section", "dp"), pairs)


def products(half, failed, counts, order, act, cot, *refs):
    outs, (acts, cots, total, sems) = refs[:-4], refs[-4:]
    section, me = lax.axis_index("section"), lax.axis_index("dp")
    flips = (0, 3 - 2 * section, 1 + 2 * section, 2)
    xs, ys, zs = ([place ^ flip for flip in flips] for place in (me % 4, me // 4 % 4, me // 16))
    fetch = [
        pltpu.make_async_copy(
            act.at[0, :, :, pl.ds(pl.multiple_of(zs[half + g] * TILE, 128), TILE)], acts.at[g], sems.at[g])
        for g in range(2)
    ]
    load = [
        pltpu.make_async_copy(cot.at[0, :, :, pl.ds(column, columns)], cots.at[:, :, pl.ds(column, columns)], sems.at[2 + c])
        for c, (column, columns, _) in enumerate(COLOURS)
    ]
    fetch[0].start()
    for copy in load:
        copy.start()
    fetch[1].start()
    alive = jnp.where(me == failed[0], 0, counts[0])
    live = [jnp.float32(0)] * SLOTS
    for position in range(SLOTS):
        for k in range(SLOTS):
            live[k] = jnp.where((order[0, position] == k) & (position < alive), jnp.float32(1), live[k])
    if half == 2:
        outs[5][...] = jnp.full((8, 128), alive.astype(jnp.float32))
    for g in range(2):
        fetch[g].wait()
        rows = acts[g].reshape(K, TILE)
        for c, (column, columns, _) in enumerate(COLOURS):
            span = slice(column, column + columns)
            if g == 0:
                load[c].wait()
                for k in range(SLOTS):
                    cots[k, :, span] = cots[k, :, span] * live[k].astype(jnp.bfloat16)
            total[:, :columns] = lax.dot_general(
                rows, cots[:, :, span].reshape(K, columns), (((0,), (0,)), ((), ())),
                preferred_element_type=jnp.float32)
            for i in range(4):
                for j in range(4):
                    if c == 0:
                        start = xs[i] * ROWS + ys[j] * 160
                    elif c == 1:
                        start = ys[i] * 160 + xs[j] * ROWS
                    else:
                        start = jnp.where(section == 0, ys[i] * 160 + xs[j] * ROWS, xs[i] * ROWS + ys[j] * 160)
                    block = total[pl.ds(pl.multiple_of(start, 8), ROWS), :columns]
                    if c == 2:
                        outs[4][g, i, j] = block
                    else:
                        outs[2 * c + i // 2][i % 2, j, g] = block


def partials(half, activations, cotangents, failed, counts, order):
    shapes = [jax.ShapeDtypeStruct((2, 4, 2, ROWS, 768), jnp.float32)] * 4
    shapes.append(jax.ShapeDtypeStruct((2, 4, 4, ROWS, 1024), jnp.float32))
    if half == 2:
        shapes.append(jax.ShapeDtypeStruct((8, 128), jnp.float32))
    return pl.pallas_call(
        functools.partial(products, half),
        out_shape=shapes,
        in_specs=[pl.BlockSpec(memory_space=pltpu.SMEM)] * 3 + [pl.BlockSpec(memory_space=pltpu.HBM)] * 2,
        out_specs=[pl.BlockSpec(memory_space=pltpu.VMEM)] * len(shapes),
        scratch_shapes=[
            pltpu.VMEM((2, SLOTS, TOKENS, TILE), jnp.bfloat16),
            pltpu.VMEM((SLOTS, TOKENS, 2560), jnp.bfloat16),
            pltpu.VMEM((TILE, 1024), jnp.float32),
            pltpu.SemaphoreType.DMA((5,)),
        ],
        compiler_params=pltpu.CompilerParams(vmem_limit_bytes=26 << 20),
        cost_estimate=pl.CostEstimate(flops=1024, bytes_accessed=1024, transcendentals=0),
    )(failed, counts, order, *(pltpu.with_memory_space_constraint(x, pltpu.HBM) for x in (activations, cotangents)))


def together(values):
    return list(lax.optimization_barrier(tuple(values)))


def shards(activations, cotangents, failed, counts, order):
    axes = [[(colour[2][0][phase], colour[2][1][phase]) for colour in COLOURS] for phase in range(3)]

    def step(values, turn, phase):
        return [exchange(v, a, turn) for v, a in zip(values, axes[phase])]

    one = partials(2, activations, cotangents, failed, counts, order)
    activations, cotangents, *one = together([activations, cotangents, *one])
    two = partials(0, activations, cotangents, failed, counts, order)
    count = one[5]

    def counted(values, turn, axis):
        nonlocal count
        *values, got = together([*values, exchange(count, (axis, axis), turn)])
        count = count + got
        return values

    got_far = step([one[1], one[3]], 0, 0)
    got_near = step([two[1], two[3], one[4]], 0, 0)
    keep_far = [one[0], one[2], two[4][:, :, 2:4]]
    keep_near = [two[0], two[2], two[4][:, :, 0:2]]
    got_far = counted(got_far, 0, "x")
    got_near = counted(got_near, 1, "x")
    got_far.append(got_near[2][:, :, 2:4])
    got_near[2] = got_near[2][:, :, 0:2]
    keep, got = [keep_far, keep_near], [got_far, got_near]
    late = [step([k[1] + r[1] for k, r in zip(keep[i], got[i])], 1, 0) for i in range(2)]
    late = [counted(late[i], i, "y") for i in range(2)]
    whole = [[k[0] + r[0] + s for k, r, s in zip(keep[i], got[i], late[i])] for i in range(2)]
    send = [[w[2:4] for w in whole[i]] for i in range(2)]
    keep = [[w[0:2] for w in whole[i]] for i in range(2)]
    got = [counted(step(send[i], 0, 1), i, "z") for i in range(2)]
    late = [together(step([k[1] + r[1] for k, r in zip(keep[i], got[i])], 1, 1)) for i in range(2)]
    far, near = [[k[0] + r[0] + s for k, r, s in zip(keep[i], got[i], late[i])] for i in range(2)]
    got = together(step(far, 0, 2))
    late = together(step([k[1] + r[1] for k, r in zip(near, got)], 1, 2))
    total = count[0, 0]
    return jnp.concatenate([(k[0] + r[0] + s) / total for k, r, s in zip(near, got, late)], axis=1)


def solution(mesh):
    in_specs = (
        P(("section", "dp"), None, None, None),
        P(("section", "dp"), None, None, None),
        P(),
        P("dp"),
        P("dp", None),
    )
    out_specs = P(("section", "dp"), None)
    return jax.shard_map(shards, mesh=mesh, in_specs=in_specs, out_specs=out_specs, check_vma=False)
```

```python
import functools

import jax
import jax.numpy as jnp
from jax import lax
from jax.experimental import pallas as pl
from jax.experimental.pallas import tpu as pltpu
from jax.sharding import PartitionSpec as P

SLOTS, TOKENS, ROWS = 6, 192, 40
K = SLOTS * TOKENS
TILE = 16 * ROWS
STRIDE = {"x": 1, "y": 4, "z": 16}
COLUMNS = {"A": (0, 896), "B": (896, 896), "C": (1792, 768)}


def exchange(value, axis, turn):
    pairs = []
    for section in range(2):
        flip, stride = 1 if section == turn else 3, STRIDE[axis]
        for d in range(64):
            p = d // stride % 4
            pairs.append((section * 64 + d, section * 64 + d + ((p ^ flip) - p) * stride))
    return lax.ppermute(value, ("section", "dp"), pairs)


def products(half, groups, failed, counts, order, act, cot, *refs):
    outs, (acts, cots, total, sems) = list(refs[:-4]), refs[-4:]
    section, me = lax.axis_index("section"), lax.axis_index("dp")
    flips = (0, 3 - 2 * section, 1 + 2 * section, 2)
    xs, ys, zs = ([place ^ flip for flip in flips] for place in (me % 4, me // 4 % 4, me // 16))
    first = COLUMNS[groups[0]][0]
    fetch = [
        pltpu.make_async_copy(
            act.at[0, :, :, pl.ds(pl.multiple_of(zs[half + g] * TILE, 128), TILE)], acts.at[g], sems.at[g])
        for g in range(2)
    ]
    load = {}
    for n, group in enumerate(groups):
        column, columns = COLUMNS[group]
        load[group] = pltpu.make_async_copy(
            cot.at[0, :, :, pl.ds(column, columns)], cots.at[:, :, pl.ds(column - first, columns)], sems.at[2 + n])
    fetch[0].start()
    for copy in load.values():
        copy.start()
    fetch[1].start()
    alive = jnp.where(me == failed[0], 0, counts[0])
    live = [jnp.float32(0)] * SLOTS
    for position in range(SLOTS):
        for k in range(SLOTS):
            live[k] = jnp.where((order[0, position] == k) & (position < alive), jnp.float32(1), live[k])
    targets = {group: [outs.pop(0), outs.pop(0)] if group in "AB" else [outs.pop(0)] for group in groups}
    if half == 2 and "C" in groups:
        alive_rows = jnp.full((8, COLUMNS["C"][1]), alive.astype(jnp.float32))
        targets["C"][0][2 * TILE:, :] = alive_rows
        outs.pop(0)[...] = alive_rows
    for g in range(2):
        fetch[g].wait()
        rows = acts[g].reshape(K, TILE)
        for group in groups:
            column, columns = COLUMNS[group]
            span = slice(column - first, column - first + columns)
            if g == 0:
                load[group].wait()
                for k in range(SLOTS):
                    cots[k, :, span] = cots[k, :, span] * live[k].astype(jnp.bfloat16)
            total[:, :columns] = lax.dot_general(
                rows, cots[:, :, span].reshape(K, columns), (((0,), (0,)), ((), ())),
                preferred_element_type=jnp.float32)
            for i in range(4):
                for j in range(4):
                    start = ys[i] * 160 + xs[j] * ROWS if group == "B" else xs[i] * ROWS + ys[j] * 160
                    block = total[pl.ds(pl.multiple_of(start, 8), ROWS), :columns]
                    if group == "A":
                        targets["A"][i // 2][i % 2, j, g] = block
                    elif group == "B":
                        targets["B"][i // 2][i % 2, g, j] = block
                    else:
                        targets["C"][0][pl.ds(((g * 4 + i) * 4 + j) * ROWS, ROWS), :] = block


def partials(half, groups, activations, cotangents, failed, counts, order):
    f32 = lambda *shape: jax.ShapeDtypeStruct(shape, jnp.float32)
    shapes = []
    for group in groups:
        columns = COLUMNS[group][1]
        if group == "A":
            shapes += [f32(2, 4, 2, ROWS, columns)] * 2
        elif group == "B":
            shapes += [f32(2, 2, 4, ROWS, columns)] * 2
        elif half == 2:
            shapes += [f32(2 * TILE + 8, columns), f32(8, columns)]
        else:
            shapes += [f32(2 * TILE, columns)]
    return pl.pallas_call(
        functools.partial(products, half, groups),
        out_shape=shapes,
        in_specs=[pl.BlockSpec(memory_space=pltpu.SMEM)] * 3 + [pl.BlockSpec(memory_space=pltpu.HBM)] * 2,
        out_specs=[pl.BlockSpec(memory_space=pltpu.VMEM)] * len(shapes),
        scratch_shapes=[
            pltpu.VMEM((2, SLOTS, TOKENS, TILE), jnp.bfloat16),
            pltpu.VMEM((SLOTS, TOKENS, sum(COLUMNS[group][1] for group in groups)), jnp.bfloat16),
            pltpu.VMEM((TILE, max(COLUMNS[group][1] for group in groups)), jnp.float32),
            pltpu.SemaphoreType.DMA((5,)),
        ],
        compiler_params=pltpu.CompilerParams(vmem_limit_bytes=27 << 20),
        cost_estimate=pl.CostEstimate(flops=1024, bytes_accessed=1024, transcendentals=0),
    )(failed, counts, order, *(pltpu.with_memory_space_constraint(x, pltpu.HBM) for x in (activations, cotangents)))


def together(values):
    return list(lax.optimization_barrier(tuple(values)))


def shards(activations, cotangents, failed, counts, order):
    run = functools.partial(partials, failed=failed, counts=counts, order=order)
    *one, activations, cotangents = together([*run(2, "ABC", activations, cotangents), activations, cotangents])
    a_keep_far, a_send_far, b_keep_far, b_send_far, c_send, c_total = one
    a_keep_near, a_send_near, b_keep_near, b_send_near, c_keep = run(0, "ABC", activations, cotangents)

    def both(keep, got, total, rows):
        total = total + got[2 * rows:]
        return jnp.concatenate([keep[rows:] + got[rows:2 * rows], total], axis=0), keep[:rows] + got[:rows], total

    a_got_far, b_got_far = together([exchange(a_send_far, "x", 0), exchange(b_send_far, "y", 0)])
    a_got_near, b_got_near, c_got = together(
        [exchange(a_send_near, "x", 0), exchange(b_send_near, "y", 0), exchange(c_send, "z", 0)])
    a_late_far, b_late_far = together(
        [exchange(a_keep_far[1] + a_got_far[1], "x", 1), exchange(b_keep_far[1] + b_got_far[1], "y", 1)])
    c_out, c_stay, c_total = both(c_keep, c_got, c_total, TILE)
    a_late_near, b_late_near, c_late = together([
        exchange(a_keep_near[1] + a_got_near[1], "x", 1), exchange(b_keep_near[1] + b_got_near[1], "y", 1),
        exchange(c_out, "z", 1)])
    c_whole, c_total = c_stay + c_late[:TILE], c_total + c_late[TILE:]

    a_far = (a_keep_far[0] + a_got_far[0]) + a_late_far
    b_far = (b_keep_far[0] + b_got_far[0]) + b_late_far
    a_near = (a_keep_near[0] + a_got_near[0]) + a_late_near
    b_near = (b_keep_near[0] + b_got_near[0]) + b_late_near
    a_got_far, b_got = together([exchange(a_far[2:4], "y", 0), exchange(b_far, "z", 0)])
    a_got_near, c_got = together([
        exchange(a_near[2:4], "y", 0), exchange(jnp.concatenate([c_whole[320:], c_total], axis=0), "x", 0)])
    a_late = exchange(jnp.concatenate([a_far[1] + a_got_far[1], a_near[1] + a_got_near[1]], axis=0), "y", 1)
    b_late = exchange(b_near[1] + b_got[1], "z", 1)
    c_out, c_stay, c_total = both(c_whole[:320], c_got, c_total, 160)
    c_late = exchange(c_out, "x", 1)
    a_late, b_late, c_late = together([a_late, b_late, c_late])
    c_whole, c_total = c_stay + c_late[:160], c_total + c_late[160:]
    a_far, a_near = (a_far[0] + a_got_far[0]) + a_late[:2], (a_near[0] + a_got_near[0]) + a_late[2:]
    b_whole = (b_near[0] + b_got[0]) + b_late

    a_got, b_got = exchange(a_far, "z", 0), exchange(b_whole[2:4], "x", 0)
    c_got = exchange(jnp.concatenate([c_whole[80:], c_total], axis=0), "y", 0)
    a_got, b_got, c_got = together([a_got, b_got, c_got])
    a_late = exchange(a_near[1] + a_got[1], "z", 1)
    b_late = exchange(b_whole[1] + b_got[1], "x", 1)
    c_out, c_stay, c_total = both(c_whole[:80], c_got, c_total, 40)
    c_late = exchange(c_out, "y", 1)
    a_late, b_late, c_late = together([a_late, b_late, c_late])
    a = (a_near[0] + a_got[0]) + a_late
    b = (b_whole[0] + b_got[0]) + b_late
    c = c_stay + c_late[:40]
    total = (c_total + c_late[40:])[0, 0]
    return jnp.concatenate([a / total, b / total, c / total], axis=1)


def solution(mesh):
    in_specs = (
        P(("section", "dp"), None, None, None),
        P(("section", "dp"), None, None, None),
        P(),
        P("dp"),
        P("dp", None),
    )
    out_specs = P(("section", "dp"), None)
    return jax.shard_map(shards, mesh=mesh, in_specs=in_specs, out_specs=out_specs, check_vma=False)
```

```python
import functools

import jax
import jax.numpy as jnp
from jax import lax
from jax.experimental import pallas as pl
from jax.experimental.pallas import tpu as pltpu
from jax.sharding import PartitionSpec as P

SLOTS, TOKENS, ROWS = 6, 192, 40
K = SLOTS * TOKENS
TILE = 16 * ROWS
STRIDE = {"x": 1, "y": 4, "z": 16}
COLUMNS = {"A": (0, 896), "B": (896, 896), "C": (1792, 768)}


def exchange(value, axis, turn):
    pairs = []
    for section in range(2):
        flip, stride = 1 if section == turn else 3, STRIDE[axis]
        for d in range(64):
            p = d // stride % 4
            pairs.append((section * 64 + d, section * 64 + d + ((p ^ flip) - p) * stride))
    return lax.ppermute(value, ("section", "dp"), pairs)


def products(half, failed, counts, order, act, cot, *refs):
    outs, (acts, cots, total, sems) = refs[:-4], refs[-4:]
    section, me = lax.axis_index("section"), lax.axis_index("dp")
    flips = (0, 3 - 2 * section, 1 + 2 * section, 2)
    xs, ys, zs = ([place ^ flip for flip in flips] for place in (me % 4, me // 4 % 4, me // 16))
    fetch = [
        pltpu.make_async_copy(
            act.at[0, :, :, pl.ds(pl.multiple_of(zs[half + g] * TILE, 128), TILE)], acts.at[g], sems.at[g])
        for g in range(2)
    ]
    load = {}
    for n, pack in enumerate(("AB", "C")):
        span = pl.ds(COLUMNS[pack[0]][0], sum(COLUMNS[pack[-1]]) - COLUMNS[pack[0]][0])
        load[pack] = pltpu.make_async_copy(cot.at[0, :, :, span], cots.at[:, :, span], sems.at[2 + n])
    fetch[0].start()
    for copy in load.values():
        copy.start()
    fetch[1].start()
    alive = jnp.where(me == failed[0], 0, counts[0])
    live = [jnp.float32(0)] * SLOTS
    for position in range(SLOTS):
        for k in range(SLOTS):
            live[k] = jnp.where((order[0, position] == k) & (position < alive), jnp.float32(1), live[k])
    if half == 2:
        alive_rows = jnp.full((8, COLUMNS["C"][1]), alive.astype(jnp.float32))
        outs[4][2 * TILE:, :] = alive_rows
        outs[5][...] = alive_rows
    for g in range(2):
        fetch[g].wait()
        rows = acts[g].reshape(K, TILE)
        for pack in ("AB", "C"):
            first, last = COLUMNS[pack[0]][0], sum(COLUMNS[pack[-1]])
            if g == 0:
                load[pack].wait()
                for k in range(SLOTS):
                    cots[k, :, first:last] = cots[k, :, first:last] * live[k].astype(jnp.bfloat16)
            total[:, :last - first] = lax.dot_general(
                rows, cots[:, :, first:last].reshape(K, last - first), (((0,), (0,)), ((), ())),
                preferred_element_type=jnp.float32)
            for group in pack:
                column, columns = COLUMNS[group]
                for i in range(4):
                    for j in range(4):
                        start = ys[i] * 160 + xs[j] * ROWS if group == "B" else xs[i] * ROWS + ys[j] * 160
                        block = total[pl.ds(pl.multiple_of(start, 8), ROWS), column - first:column - first + columns]
                        if group == "A":
                            outs[i // 2][i % 2, j, g] = block
                        elif group == "B":
                            outs[2 + i // 2][i % 2, g, j] = block
                        else:
                            outs[4][pl.ds(((g * 4 + i) * 4 + j) * ROWS, ROWS), :] = block


def partials(half, activations, cotangents, failed, counts, order):
    a, b, c = (COLUMNS[group][1] for group in "ABC")
    shapes = [(2, 4, 2, ROWS, a)] * 2 + [(2, 2, 4, ROWS, b)] * 2
    shapes += [(2 * TILE + 8, c), (8, c)] if half == 2 else [(2 * TILE, c)]
    return pl.pallas_call(
        functools.partial(products, half),
        out_shape=[jax.ShapeDtypeStruct(shape, jnp.float32) for shape in shapes],
        in_specs=[pl.BlockSpec(memory_space=pltpu.SMEM)] * 3 + [pl.BlockSpec(memory_space=pltpu.HBM)] * 2,
        out_specs=[pl.BlockSpec(memory_space=pltpu.VMEM)] * len(shapes),
        scratch_shapes=[
            pltpu.VMEM((2, SLOTS, TOKENS, TILE), jnp.bfloat16),
            pltpu.VMEM((SLOTS, TOKENS, a + b + c), jnp.bfloat16),
            pltpu.VMEM((TILE, max(a + b, c)), jnp.float32),
            pltpu.SemaphoreType.DMA((4,)),
        ],
        compiler_params=pltpu.CompilerParams(vmem_limit_bytes=28 << 20),
        cost_estimate=pl.CostEstimate(flops=1024, bytes_accessed=1024, transcendentals=0),
    )(failed, counts, order, *(pltpu.with_memory_space_constraint(x, pltpu.HBM) for x in (activations, cotangents)))


def together(values):
    return list(lax.optimization_barrier(tuple(values)))


def shards(activations, cotangents, failed, counts, order):
    run = functools.partial(partials, failed=failed, counts=counts, order=order)
    *one, activations, cotangents = together([*run(2, activations, cotangents), activations, cotangents])
    a_keep_far, a_send_far, b_keep_far, b_send_far, c_send, c_total = one
    a_keep_near, a_send_near, b_keep_near, b_send_near, c_keep = run(0, activations, cotangents)
    taken = None

    def take(got):
        nonlocal taken
        taken = got if taken is None else together([got, taken])[0]
        return taken

    def both(keep, got, total, rows):
        total = total + got[2 * rows:]
        return jnp.concatenate([keep[rows:] + got[rows:2 * rows], total], axis=0), keep[:rows] + got[:rows], total

    a1f, b1f, c1 = exchange(a_send_far, "x", 0), exchange(b_send_far, "y", 0), exchange(c_send, "z", 0)
    a1n, b1n = exchange(a_send_near, "x", 0), exchange(b_send_near, "y", 0)
    a1f = take(a1f)
    a2f = exchange(a_keep_far[1] + a1f[1], "x", 1)
    b1f = take(b1f)
    b2f = exchange(b_keep_far[1] + b1f[1], "y", 1)
    c1 = take(c1)
    c_out, c_stay, c_total = both(c_keep, c1, c_total, TILE)
    c2 = exchange(c_out, "z", 1)
    a1n = take(a1n)
    a2n = exchange(a_keep_near[1] + a1n[1], "x", 1)
    b1n = take(b1n)
    b2n = exchange(b_keep_near[1] + b1n[1], "y", 1)
    a2f = take(a2f)
    a_far = (a_keep_far[0] + a1f[0]) + a2f
    a3f = exchange(a_far[2:4], "y", 0)
    b2f = take(b2f)
    b_far = (b_keep_far[0] + b1f[0]) + b2f
    b3 = exchange(b_far, "z", 0)
    c2 = take(c2)
    c_whole, c_total = c_stay + c2[:TILE], c_total + c2[TILE:]
    c3 = exchange(jnp.concatenate([c_whole[320:], c_total], axis=0), "x", 0)
    a2n = take(a2n)
    a_near = (a_keep_near[0] + a1n[0]) + a2n
    a3n = exchange(a_near[2:4], "y", 0)
    b2n = take(b2n)
    b_near = (b_keep_near[0] + b1n[0]) + b2n
    a3f = take(a3f)
    b3 = take(b3)
    b4 = exchange(b_near[1] + b3[1], "z", 1)
    c3 = take(c3)
    c_out, c_stay, c_total = both(c_whole[:320], c3, c_total, 160)
    c4 = exchange(c_out, "x", 1)
    a3n = take(a3n)
    a4 = exchange(jnp.concatenate([a_far[1] + a3f[1], a_near[1] + a3n[1]], axis=0), "y", 1)
    b4 = take(b4)
    b_whole = (b_near[0] + b3[0]) + b4
    b5 = exchange(b_whole[2:4], "x", 0)
    c4 = take(c4)
    c_whole, c_total = c_stay + c4[:160], c_total + c4[160:]
    c5 = exchange(jnp.concatenate([c_whole[80:], c_total], axis=0), "y", 0)
    a4 = take(a4)
    a_far, a_near = (a_far[0] + a3f[0]) + a4[:2], (a_near[0] + a3n[0]) + a4[2:]
    a5 = exchange(a_far, "z", 0)
    b5 = take(b5)
    b6 = exchange(b_whole[1] + b5[1], "x", 1)
    c5 = take(c5)
    c_out, c_stay, c_total = both(c_whole[:80], c5, c_total, 40)
    c6 = exchange(c_out, "y", 1)
    a5 = take(a5)
    a6 = exchange(a_near[1] + a5[1], "z", 1)
    b6, c6, a6 = together([b6, c6, a6])
    a = (a_near[0] + a5[0]) + a6
    b = (b_whole[0] + b5[0]) + b6
    c = c_stay + c6[:40]
    total = (c_total + c6[40:])[0, 0]
    return jnp.concatenate([a / total, b / total, c / total], axis=1)


def solution(mesh):
    in_specs = (
        P(("section", "dp"), None, None, None),
        P(("section", "dp"), None, None, None),
        P(),
        P("dp"),
        P("dp", None),
    )
    out_specs = P(("section", "dp"), None)
    return jax.shard_map(shards, mesh=mesh, in_specs=in_specs, out_specs=out_specs, check_vma=False)
```

```python
import functools

import jax
import jax.numpy as jnp
from jax import lax
from jax.experimental import pallas as pl
from jax.experimental.pallas import tpu as pltpu
from jax.sharding import PartitionSpec as P

SLOTS, TOKENS, ROWS = 6, 192, 40
K = SLOTS * TOKENS
TILE = 16 * ROWS
STRIDE = {"x": 1, "y": 4, "z": 16}
COLUMNS = {"A": (0, 896), "B": (896, 896), "C": (1792, 768)}


def exchange(value, axis, turn):
    pairs = []
    for section in range(2):
        flip, stride = 1 if section == turn else 3, STRIDE[axis]
        for d in range(64):
            p = d // stride % 4
            pairs.append((section * 64 + d, section * 64 + d + ((p ^ flip) - p) * stride))
    return lax.ppermute(value, ("section", "dp"), pairs)


def masked(failed, counts, order, cots):
    me = lax.axis_index("dp")
    alive = jnp.where(me == failed[0], 0, counts[0])
    for k in range(SLOTS):
        live = jnp.float32(0)
        for position in range(SLOTS):
            live = jnp.where((order[0, position] == k) & (position < alive), jnp.float32(1), live)
        cots[k] = cots[k] * live.astype(jnp.bfloat16)
    return alive.astype(jnp.float32)


def product(rows, cots):
    return lax.dot_general(
        rows.reshape(K, TILE), cots[...].reshape(K, cots.shape[2]), (((0,), (0,)), ((), ())),
        preferred_element_type=jnp.float32)


def whole_products(failed, counts, order, act, cot, out, acts, cots, total, sems):
    column, columns = COLUMNS["C"]
    load = pltpu.make_async_copy(cot.at[0, :, :, pl.ds(column, columns)], cots, sems.at[0])
    fetch = [
        pltpu.make_async_copy(act.at[0, :, :, pl.ds(g * TILE, TILE)], acts.at[g], sems.at[1 + g]) for g in range(4)
    ]
    store = [pltpu.make_async_copy(total.at[g], out.at[pl.ds(g * TILE, TILE), :], sems.at[5 + g]) for g in range(4)]
    load.start()
    for copy in fetch:
        copy.start()
    load.wait()
    masked(failed, counts, order, cots)
    for g in range(4):
        fetch[g].wait()
        total[g] = product(acts[g], cots)
        store[g].start()
    for copy in store:
        copy.wait()


def products(half, failed, counts, order, act, cot, *refs):
    (a_keep, a_send, b_keep, b_send), (acts, cots, total, sems) = refs[:4], refs[-4:]
    section, me = lax.axis_index("section"), lax.axis_index("dp")
    flips = (0, 3 - 2 * section, 1 + 2 * section, 2)
    xs, ys, zs = ([place ^ flip for flip in flips] for place in (me % 4, me // 4 % 4, me // 16))
    width = COLUMNS["B"][0]
    load = pltpu.make_async_copy(cot.at[0, :, :, pl.ds(0, 2 * width)], cots, sems.at[0])
    fetch = [
        pltpu.make_async_copy(
            act.at[0, :, :, pl.ds(pl.multiple_of(zs[half + g] * TILE, 128), TILE)], acts.at[g], sems.at[1 + g])
        for g in range(2)
    ]
    load.start()
    for copy in fetch:
        copy.start()
    load.wait()
    alive = masked(failed, counts, order, cots)
    if half == 2:
        alive_rows = jnp.full((8, width), alive)
        b_send[TILE:, :] = alive_rows
        refs[4][...] = alive_rows
    for g in range(2):
        fetch[g].wait()
        total[...] = product(acts[g], cots)
        for i in range(4):
            for j in range(4):
                rows = pl.ds(pl.multiple_of(xs[i] * ROWS + ys[j] * 160, 8), ROWS)
                (a_keep if i < 2 else a_send)[i % 2, j, g] = total[rows, :width]
                rows = pl.ds(pl.multiple_of(ys[i] * 160 + xs[j] * ROWS, 8), ROWS)
                (b_keep if i < 2 else b_send)[pl.ds(((i % 2 * 2 + g) * 4 + j) * ROWS, ROWS), :] = total[rows, width:]


def call(kernel, shapes, out_space, scratch, limit, activations, cotangents, failed, counts, order):
    return pl.pallas_call(
        kernel,
        out_shape=[pltpu.HBM(shape, jnp.float32) if out_space == pltpu.HBM else jax.ShapeDtypeStruct(shape, jnp.float32) for shape in shapes],
        in_specs=[pl.BlockSpec(memory_space=pltpu.SMEM)] * 3 + [pl.BlockSpec(memory_space=pltpu.HBM)] * 2,
        out_specs=[pl.BlockSpec(memory_space=out_space)] * len(shapes),
        scratch_shapes=scratch,
        compiler_params=pltpu.CompilerParams(vmem_limit_bytes=limit << 20),
        cost_estimate=pl.CostEstimate(flops=1024, bytes_accessed=1024, transcendentals=0),
    )(failed, counts, order, *(pltpu.with_memory_space_constraint(x, pltpu.HBM) for x in (activations, cotangents)))


def partials(half, *args):
    width = COLUMNS["B"][0]
    shapes = [(2, 4, 2, ROWS, width)] * 2 + [(TILE, width), (TILE + 8, width) if half == 2 else (TILE, width)]
    shapes += [(8, width)] if half == 2 else []
    scratch = [
        pltpu.VMEM((2, SLOTS, TOKENS, TILE), jnp.bfloat16),
        pltpu.VMEM((SLOTS, TOKENS, 2 * width), jnp.bfloat16),
        pltpu.VMEM((TILE, 2 * width), jnp.float32),
        pltpu.SemaphoreType.DMA((3,)),
    ]
    return call(functools.partial(products, half), shapes, pltpu.VMEM, scratch, 22, *args)


def whole_partial(*args):
    columns = COLUMNS["C"][1]
    scratch = [
        pltpu.VMEM((4, SLOTS, TOKENS, TILE), jnp.bfloat16),
        pltpu.VMEM((SLOTS, TOKENS, columns), jnp.bfloat16),
        pltpu.VMEM((4, TILE, columns), jnp.float32),
        pltpu.SemaphoreType.DMA((9,)),
    ]
    return call(whole_products, [(4 * TILE, columns)], pltpu.HBM, scratch, 22, *args)[0]


def together(values):
    return list(lax.optimization_barrier(tuple(values)))


def shards(activations, cotangents, failed, counts, order):
    c = whole_partial(activations, cotangents, failed, counts, order)
    c, activations, cotangents = together([c, activations, cotangents])
    c = lax.psum_scatter(
        c, "dp", scatter_dimension=0, tiled=True, axis_index_groups=[[d + 16 * z for z in range(4)] for d in range(16)])
    c = lax.psum_scatter(
        c, "dp", scatter_dimension=0, tiled=True, axis_index_groups=[[d + 16 * z for d in range(16)] for z in range(4)])
    *one, activations, cotangents = together(
        [*partials(2, activations, cotangents, failed, counts, order), activations, cotangents])
    a_keep_far, a_send_far, b_keep_far, b_send_far, total = one
    a_keep_near, a_send_near, b_keep_near, b_send_near = partials(0, activations, cotangents, failed, counts, order)
    taken = None

    def take(got):
        nonlocal taken
        taken = got if taken is None else together([got, taken])[0]
        return taken

    def under(rows, total):
        return jnp.concatenate([rows, total], axis=0)

    a1f, b1f = exchange(a_send_far, "x", 0), exchange(b_send_far, "y", 0)
    a1n, b1n = exchange(a_send_near, "x", 0), exchange(b_send_near, "y", 0)
    a1f = take(a1f)
    a2f = exchange(a_keep_far[1] + a1f[1], "x", 1)
    b1f = take(b1f)
    total = total + b1f[640:]
    b2f = exchange(under(b_keep_far[320:] + b1f[320:640], total), "y", 1)
    a1n = take(a1n)
    a2n = exchange(a_keep_near[1] + a1n[1], "x", 1)
    b1n = take(b1n)
    b2n = exchange(b_keep_near[320:] + b1n[320:], "y", 1)
    a2f = take(a2f)
    a_far = (a_keep_far[0] + a1f[0]) + a2f
    a3f = exchange(a_far[2:4], "y", 0)
    b2f = take(b2f)
    total = total + b2f[320:]
    b3 = exchange(under((b_keep_far[:320] + b1f[:320]) + b2f[:320], total), "z", 0)
    a2n = take(a2n)
    a_near = (a_keep_near[0] + a1n[0]) + a2n
    a3n = exchange(a_near[2:4], "y", 0)
    b2n = take(b2n)
    b_near = (b_keep_near[:320] + b1n[:320]) + b2n
    b3 = take(b3)
    total = total + b3[320:]
    b4 = exchange(under(b_near[160:] + b3[160:320], total), "z", 1)
    a3f = take(a3f)
    a3n = take(a3n)
    a4 = exchange(jnp.concatenate([a_far[1] + a3f[1], a_near[1] + a3n[1]], axis=0), "y", 1)
    b4 = take(b4)
    total = total + b4[160:]
    b_whole = (b_near[:160] + b3[:160]) + b4[:160]
    b5 = exchange(under(b_whole[80:], total), "x", 0)
    a4 = take(a4)
    a_far, a_near = (a_far[0] + a3f[0]) + a4[:2], (a_near[0] + a3n[0]) + a4[2:]
    a5 = exchange(a_far, "z", 0)
    b5 = take(b5)
    total = total + b5[80:]
    b6 = exchange(under(b_whole[40:80] + b5[40:80], total), "x", 1)
    a5 = take(a5)
    a6 = exchange(a_near[1] + a5[1], "z", 1)
    b6, a6, c = together([b6, a6, c])
    a = (a_near[0] + a5[0]) + a6
    b = (b_whole[:40] + b5[:40]) + b6[:40]
    total = (total + b6[40:])[0, 0]
    return jnp.concatenate([a / total, b / total, c / total], axis=1)


def solution(mesh):
    in_specs = (
        P(("section", "dp"), None, None, None),
        P(("section", "dp"), None, None, None),
        P(),
        P("dp"),
        P("dp", None),
    )
    out_specs = P(("section", "dp"), None)
    return jax.shard_map(shards, mesh=mesh, in_specs=in_specs, out_specs=out_specs, check_vma=False)
```

```python
import functools

import jax
import jax.numpy as jnp
from jax import lax
from jax.experimental import pallas as pl
from jax.experimental.pallas import tpu as pltpu
from jax.sharding import PartitionSpec as P

SLOTS, TOKENS, ROWS = 6, 192, 40
K = SLOTS * TOKENS
TILE = 16 * ROWS
STRIDE = {"x": 1, "y": 4, "z": 16}
COLUMNS = {"A": (0, 896), "B": (896, 896), "C": (1792, 768)}


def exchange(value, axis, turn):
    pairs = []
    for section in range(2):
        flip, stride = 1 if section == turn else 3, STRIDE[axis]
        for d in range(64):
            p = d // stride % 4
            pairs.append((section * 64 + d, section * 64 + d + ((p ^ flip) - p) * stride))
    return lax.ppermute(value, ("section", "dp"), pairs)


def products(half, failed, counts, order, act, cot, *refs):
    outs, (acts, cots, total, sems) = refs[:-4], refs[-4:]
    section, me = lax.axis_index("section"), lax.axis_index("dp")
    flips = (0, 3 - 2 * section, 1 + 2 * section, 2)
    xs, ys, zs = ([place ^ flip for flip in flips] for place in (me % 4, me // 4 % 4, me // 16))
    fetch = [
        pltpu.make_async_copy(
            act.at[0, :, :, pl.ds(pl.multiple_of(zs[half + g] * TILE, 128), TILE)], acts.at[g], sems.at[g])
        for g in range(2)
    ]
    load = {}
    for n, pack in enumerate(("AB", "C")):
        span = pl.ds(COLUMNS[pack[0]][0], sum(COLUMNS[pack[-1]]) - COLUMNS[pack[0]][0])
        load[pack] = pltpu.make_async_copy(cot.at[0, :, :, span], cots.at[:, :, span], sems.at[2 + n])
    fetch[0].start()
    for copy in load.values():
        copy.start()
    fetch[1].start()
    alive = jnp.where(me == failed[0], 0, counts[0])
    live = [jnp.float32(0)] * SLOTS
    for position in range(SLOTS):
        for k in range(SLOTS):
            live[k] = jnp.where((order[0, position] == k) & (position < alive), jnp.float32(1), live[k])
    if half == 2:
        alive_rows = jnp.full((8, COLUMNS["C"][1]), alive.astype(jnp.float32))
        outs[4][2 * TILE:, :] = alive_rows
        outs[5][...] = alive_rows
    for g in range(2):
        fetch[g].wait()
        rows = acts[g].reshape(K, TILE)
        for pack in ("AB", "C"):
            first, last = COLUMNS[pack[0]][0], sum(COLUMNS[pack[-1]])
            if g == 0:
                load[pack].wait()
                for k in range(SLOTS):
                    cots[k, :, first:last] = cots[k, :, first:last] * live[k].astype(jnp.bfloat16)
            total[:, :last - first] = lax.dot_general(
                rows, cots[:, :, first:last].reshape(K, last - first), (((0,), (0,)), ((), ())),
                preferred_element_type=jnp.float32)
            for group in pack:
                column, columns = COLUMNS[group]
                for i in range(4):
                    for j in range(4):
                        start = ys[i] * 160 + xs[j] * ROWS if group == "B" else xs[i] * ROWS + ys[j] * 160
                        block = total[pl.ds(pl.multiple_of(start, 8), ROWS), column - first:column - first + columns]
                        if group == "A":
                            outs[i // 2][i % 2, j, g] = block
                        elif group == "B":
                            outs[2 + i // 2][i % 2, g, j] = block
                        else:
                            outs[4][pl.ds(((g * 4 + i) * 4 + j) * ROWS, ROWS), :] = block


def partials(half, activations, cotangents, failed, counts, order):
    a, b, c = (COLUMNS[group][1] for group in "ABC")
    shapes = [(2, 4, 2, ROWS, a)] * 2 + [(2, 2, 4, ROWS, b)] * 2
    shapes += [(2 * TILE + 8, c), (8, c)] if half == 2 else [(2 * TILE, c)]
    return pl.pallas_call(
        functools.partial(products, half),
        out_shape=[jax.ShapeDtypeStruct(shape, jnp.float32) for shape in shapes],
        in_specs=[pl.BlockSpec(memory_space=pltpu.SMEM)] * 3 + [pl.BlockSpec(memory_space=pltpu.HBM)] * 2,
        out_specs=[pl.BlockSpec(memory_space=pltpu.VMEM)] * len(shapes),
        scratch_shapes=[
            pltpu.VMEM((2, SLOTS, TOKENS, TILE), jnp.bfloat16),
            pltpu.VMEM((SLOTS, TOKENS, a + b + c), jnp.bfloat16),
            pltpu.VMEM((TILE, max(a + b, c)), jnp.float32),
            pltpu.SemaphoreType.DMA((4,)),
        ],
        compiler_params=pltpu.CompilerParams(vmem_limit_bytes=28 << 20),
        cost_estimate=pl.CostEstimate(flops=1024, bytes_accessed=1024, transcendentals=0),
    )(failed, counts, order, *(pltpu.with_memory_space_constraint(x, pltpu.HBM) for x in (activations, cotangents)))


def together(values):
    return list(lax.optimization_barrier(tuple(values)))


def shards(activations, cotangents, failed, counts, order):
    run = functools.partial(partials, failed=failed, counts=counts, order=order)
    *one, activations, cotangents = together([*run(2, activations, cotangents), activations, cotangents])
    a_keep_far, a_send_far, b_keep_far, b_send_far, c_send, c_total = one
    a_keep_near, a_send_near, b_keep_near, b_send_near, c_keep = run(0, activations, cotangents)
    taken = None

    def take(got):
        nonlocal taken
        taken = got if taken is None else together([got, taken])[0]
        return taken

    def both(keep, got, total, rows):
        total = total + got[2 * rows:]
        return jnp.concatenate([keep[rows:] + got[rows:2 * rows], total], axis=0), keep[:rows] + got[:rows], total

    a1f, b1f, c1 = exchange(a_send_far, "x", 0), exchange(b_send_far, "y", 0), exchange(c_send, "z", 0)
    a1n, b1n = exchange(a_send_near, "x", 0), exchange(b_send_near, "y", 0)
    a1f = take(a1f)
    a2f = exchange(a_keep_far[1] + a1f[1], "x", 1)
    b1f = take(b1f)
    b2f = exchange(b_keep_far[1] + b1f[1], "y", 1)
    c1 = take(c1)
    c_out, c_stay, c_total = both(c_keep, c1, c_total, TILE)
    c2 = exchange(c_out, "z", 1)
    a1n = take(a1n)
    a2n = exchange(a_keep_near[1] + a1n[1], "x", 1)
    b1n = take(b1n)
    b2n = exchange(b_keep_near[1] + b1n[1], "y", 1)
    a2f, b2f, c2, _ = together([a2f, b2f, c2, taken])
    taken = c2
    a_far = (a_keep_far[0] + a1f[0]) + a2f
    a3f = exchange(a_far[2:4], "y", 0)
    b_far = (b_keep_far[0] + b1f[0]) + b2f
    b3 = exchange(b_far, "z", 0)
    c_whole, c_total = c_stay + c2[:TILE], c_total + c2[TILE:]
    c3 = exchange(jnp.concatenate([c_whole[320:], c_total], axis=0), "x", 0)
    a2n = take(a2n)
    a_near = (a_keep_near[0] + a1n[0]) + a2n
    a3n = exchange(a_near[2:4], "y", 0)
    b2n = take(b2n)
    b_near = (b_keep_near[0] + b1n[0]) + b2n
    b3 = take(b3)
    b4 = exchange(b_near[1] + b3[1], "z", 1)
    c3 = take(c3)
    c_out, c_stay, c_total = both(c_whole[:320], c3, c_total, 160)
    c4 = exchange(c_out, "x", 1)
    a3f = take(a3f)
    a3n = take(a3n)
    a4 = exchange(jnp.concatenate([a_far[1] + a3f[1], a_near[1] + a3n[1]], axis=0), "y", 1)
    b4 = take(b4)
    b_whole = (b_near[0] + b3[0]) + b4
    b5 = exchange(b_whole[2:4], "x", 0)
    c4 = take(c4)
    c_whole, c_total = c_stay + c4[:160], c_total + c4[160:]
    c5 = exchange(jnp.concatenate([c_whole[80:], c_total], axis=0), "y", 0)
    a4 = take(a4)
    a_far, a_near = (a_far[0] + a3f[0]) + a4[:2], (a_near[0] + a3n[0]) + a4[2:]
    a5 = exchange(a_far, "z", 0)
    b5 = take(b5)
    b6 = exchange(b_whole[1] + b5[1], "x", 1)
    c5 = take(c5)
    c_out, c_stay, c_total = both(c_whole[:80], c5, c_total, 40)
    c6 = exchange(c_out, "y", 1)
    a5 = take(a5)
    a6 = exchange(a_near[1] + a5[1], "z", 1)
    b6, c6, a6 = together([b6, c6, a6])
    a = (a_near[0] + a5[0]) + a6
    b = (b_whole[0] + b5[0]) + b6
    c = c_stay + c6[:40]
    total = (c_total + c6[40:])[0, 0]
    return jnp.concatenate([a / total, b / total, c / total], axis=1)


def solution(mesh):
    in_specs = (
        P(("section", "dp"), None, None, None),
        P(("section", "dp"), None, None, None),
        P(),
        P("dp"),
        P("dp", None),
    )
    out_specs = P(("section", "dp"), None)
    return jax.shard_map(shards, mesh=mesh, in_specs=in_specs, out_specs=out_specs, check_vma=False)
```

```python
import functools

import jax
import jax.numpy as jnp
from jax import lax
from jax.experimental import pallas as pl
from jax.experimental.pallas import tpu as pltpu
from jax.sharding import PartitionSpec as P

SLOTS, TOKENS, ROWS = 6, 192, 40
K = SLOTS * TOKENS
TILE = 16 * ROWS
STRIDE = {"x": 1, "y": 4, "z": 16}
COLUMNS = {"A": (0, 896), "B": (896, 896), "C": (1792, 768)}


def exchange(value, axis, turn):
    pairs = []
    for section in range(2):
        flip, stride = 1 if section == turn else 3, STRIDE[axis]
        for d in range(64):
            p = d // stride % 4
            pairs.append((section * 64 + d, section * 64 + d + ((p ^ flip) - p) * stride))
    return lax.ppermute(value, ("section", "dp"), pairs)


def products(half, failed, counts, order, act, cot, *refs):
    outs, (acts, cots, total, asked, sems) = refs[:-5], refs[-5:]
    section, me = lax.axis_index("section"), lax.axis_index("dp")
    flips = (0, 3 - 2 * section, 1 + 2 * section, 2)
    xs, ys, zs = ([place ^ flip for flip in flips] for place in (me % 4, me // 4 % 4, me // 16))
    fetch = [
        pltpu.make_async_copy(
            act.at[0, :, :, pl.ds(pl.multiple_of(zs[half + g] * TILE, 128), TILE)], acts.at[g], sems.at[g])
        for g in range(2)
    ]
    load = {}
    for n, pack in enumerate(("C", "AB")):
        span = pl.ds(COLUMNS[pack[0]][0], sum(COLUMNS[pack[-1]]) - COLUMNS[pack[0]][0])
        load[pack] = pltpu.make_async_copy(cot.at[0, :, :, span], cots.at[:, :, span], sems.at[2 + n])
    ask = pltpu.make_async_copy(order, asked, sems.at[4])
    ask.start()
    load["C"].start()
    fetch[0].start()
    ask.wait()
    alive = jnp.where(me == failed[0], 0, counts[0])
    live = [jnp.float32(0)] * SLOTS
    for position in range(SLOTS):
        for k in range(SLOTS):
            live[k] = jnp.where((asked[0, position] == k) & (position < alive), jnp.float32(1), live[k])
    if half == 2:
        alive_rows = jnp.full((8, COLUMNS["C"][1]), alive.astype(jnp.float32))
        outs[4][2 * TILE:, :] = alive_rows
        outs[5][...] = alive_rows
    for g in range(2):
        fetch[g].wait()
        rows = acts[g].reshape(K, TILE)
        for pack in ("C", "AB"):
            first, last = COLUMNS[pack[0]][0], sum(COLUMNS[pack[-1]])
            if g == 0:
                load[pack].wait()
                if pack == "C":
                    load["AB"].start()
                    fetch[1].start()
                for k in range(SLOTS):
                    cots[k, :, first:last] = cots[k, :, first:last] * live[k].astype(jnp.bfloat16)
            total[:, :last - first] = lax.dot_general(
                rows, cots[:, :, first:last].reshape(K, last - first), (((0,), (0,)), ((), ())),
                preferred_element_type=jnp.float32)
            for group in pack:
                column, columns = COLUMNS[group]
                for i in range(4):
                    for j in range(4):
                        start = ys[i] * 160 + xs[j] * ROWS if group == "B" else xs[i] * ROWS + ys[j] * 160
                        block = total[pl.ds(pl.multiple_of(start, 8), ROWS), column - first:column - first + columns]
                        if group == "A":
                            outs[i // 2][i % 2, j, g] = block
                        elif group == "B":
                            outs[2 + i // 2][i % 2, g, j] = block
                        else:
                            outs[4][pl.ds(((g * 4 + i) * 4 + j) * ROWS, ROWS), :] = block


def partials(half, activations, cotangents, failed, counts, order):
    a, b, c = (COLUMNS[group][1] for group in "ABC")
    shapes = [(2, 4, 2, ROWS, a)] * 2 + [(2, 2, 4, ROWS, b)] * 2
    shapes += [(2 * TILE + 8, c), (8, c)] if half == 2 else [(2 * TILE, c)]
    return pl.pallas_call(
        functools.partial(products, half),
        out_shape=[jax.ShapeDtypeStruct(shape, jnp.float32) for shape in shapes],
        in_specs=[pl.BlockSpec(memory_space=pltpu.SMEM)] * 2 + [pl.BlockSpec(memory_space=pltpu.HBM)] * 3,
        out_specs=[pl.BlockSpec(memory_space=pltpu.VMEM)] * len(shapes),
        scratch_shapes=[
            pltpu.VMEM((2, SLOTS, TOKENS, TILE), jnp.bfloat16),
            pltpu.VMEM((SLOTS, TOKENS, a + b + c), jnp.bfloat16),
            pltpu.VMEM((TILE, max(a + b, c)), jnp.float32),
            pltpu.SMEM((1, SLOTS), jnp.int32),
            pltpu.SemaphoreType.DMA((5,)),
        ],
        compiler_params=pltpu.CompilerParams(vmem_limit_bytes=28 << 20),
        cost_estimate=pl.CostEstimate(flops=1024, bytes_accessed=1024, transcendentals=0),
    )(failed, counts, *(pltpu.with_memory_space_constraint(x, pltpu.HBM) for x in (order, activations, cotangents)))


def together(values):
    return list(lax.optimization_barrier(tuple(values)))


def shards(activations, cotangents, failed, counts, order):
    run = functools.partial(partials, failed=failed, counts=counts, order=order)
    *one, activations, cotangents = together([*run(2, activations, cotangents), activations, cotangents])
    a_keep_far, a_send_far, b_keep_far, b_send_far, c_send, c_total = one
    a_keep_near, a_send_near, b_keep_near, b_send_near, c_keep = run(0, activations, cotangents)
    taken = None

    def take(got):
        nonlocal taken
        taken = got if taken is None else together([got, taken])[0]
        return taken

    def both(keep, got, total, rows):
        total = total + got[2 * rows:]
        return jnp.concatenate([keep[rows:] + got[rows:2 * rows], total], axis=0), keep[:rows] + got[:rows], total

    a1f, b1f, c1 = exchange(a_send_far, "x", 0), exchange(b_send_far, "y", 0), exchange(c_send, "z", 0)
    a1n, b1n = exchange(a_send_near, "x", 0), exchange(b_send_near, "y", 0)
    a1f = take(a1f)
    a2f = exchange(a_keep_far[1] + a1f[1], "x", 1)
    b1f = take(b1f)
    b2f = exchange(b_keep_far[1] + b1f[1], "y", 1)
    c1 = take(c1)
    c_out, c_stay, c_total = both(c_keep, c1, c_total, TILE)
    c2 = exchange(c_out, "z", 1)
    a1n = take(a1n)
    a2n = exchange(a_keep_near[1] + a1n[1], "x", 1)
    b1n = take(b1n)
    b2n = exchange(b_keep_near[1] + b1n[1], "y", 1)
    a2f, b2f, c2, _ = together([a2f, b2f, c2, taken])
    taken = c2
    a_far = (a_keep_far[0] + a1f[0]) + a2f
    a3f = exchange(a_far[2:4], "y", 0)
    b_far = (b_keep_far[0] + b1f[0]) + b2f
    b3 = exchange(b_far, "z", 0)
    c_whole, c_total = c_stay + c2[:TILE], c_total + c2[TILE:]
    c3 = exchange(jnp.concatenate([c_whole[320:], c_total], axis=0), "x", 0)
    a2n = take(a2n)
    a_near = (a_keep_near[0] + a1n[0]) + a2n
    a3n = exchange(a_near[2:4], "y", 0)
    b2n = take(b2n)
    b_near = (b_keep_near[0] + b1n[0]) + b2n
    b3 = take(b3)
    b4 = exchange(b_near[1] + b3[1], "z", 1)
    c3 = take(c3)
    c_out, c_stay, c_total = both(c_whole[:320], c3, c_total, 160)
    c4 = exchange(c_out, "x", 1)
    a3f = take(a3f)
    a3n = take(a3n)
    a4 = exchange(jnp.concatenate([a_far[1] + a3f[1], a_near[1] + a3n[1]], axis=0), "y", 1)
    b4 = take(b4)
    b_whole = (b_near[0] + b3[0]) + b4
    b5 = exchange(b_whole[2:4], "x", 0)
    c4 = take(c4)
    c_whole, c_total = c_stay + c4[:160], c_total + c4[160:]
    c5 = exchange(jnp.concatenate([c_whole[80:], c_total], axis=0), "y", 0)
    a4 = take(a4)
    a_far, a_near = (a_far[0] + a3f[0]) + a4[:2], (a_near[0] + a3n[0]) + a4[2:]
    a5 = exchange(a_far, "z", 0)
    b5 = take(b5)
    b6 = exchange(b_whole[1] + b5[1], "x", 1)
    c5 = take(c5)
    c_out, c_stay, c_total = both(c_whole[:80], c5, c_total, 40)
    c6 = exchange(c_out, "y", 1)
    a5 = together([take(a5), b6])[0]
    a6 = exchange(a_near[1] + a5[1], "z", 1)
    b6, c6, a6 = together([b6, c6, a6])
    a = (a_near[0] + a5[0]) + a6
    b = (b_whole[0] + b5[0]) + b6
    c = c_stay + c6[:40]
    total = c_total + c6[40:]
    total = jnp.concatenate([total, total, total, total[:, :256]], axis=1)
    gradient = jnp.concatenate([a, b, c], axis=1)
    return (gradient.reshape(5, 8, 2560) / total).reshape(40, 2560)


def solution(mesh):
    in_specs = (
        P(("section", "dp"), None, None, None),
        P(("section", "dp"), None, None, None),
        P(),
        P("dp"),
        P("dp", None),
    )
    out_specs = P(("section", "dp"), None)
    return jax.shard_map(shards, mesh=mesh, in_specs=in_specs, out_specs=out_specs, check_vma=False)
```

```python
import functools

import jax
import jax.numpy as jnp
from jax import lax
from jax.experimental import pallas as pl
from jax.experimental.pallas import tpu as pltpu
from jax.sharding import PartitionSpec as P

SLOTS, TOKENS, ROWS = 6, 192, 40
K = SLOTS * TOKENS
TILE = 16 * ROWS
STRIDE = {"x": 1, "y": 4, "z": 16}
COLUMNS = {"A": (0, 896), "B": (896, 896), "C": (1792, 768)}


def exchange(value, axis, turn, other=False):
    pairs = []
    for section in range(2):
        flip, stride = 1 if (section == turn) != other else 3, STRIDE[axis]
        for d in range(64):
            p = d // stride % 4
            pairs.append((section * 64 + d, section * 64 + d + ((p ^ flip) - p) * stride))
    return lax.ppermute(value, ("section", "dp"), pairs)


def products(half, failed, counts, order, act, cot, *refs):
    outs, (acts, cots, total, asked, sems) = refs[:-5], refs[-5:]
    section, me = lax.axis_index("section"), lax.axis_index("dp")
    flips = (0, 3 - 2 * section, 1 + 2 * section, 2)
    others = (0, 1 + 2 * section, 3 - 2 * section, 2)
    x, y, z = me % 4, me // 4 % 4, me // 16
    zs = [z ^ flip for flip in flips]
    xs = {group: [x ^ flip for flip in (flips if group == "A" else others)] for group in "ABC"}
    ys = {group: [y ^ flip for flip in (flips if group == "B" else others)] for group in "ABC"}
    fetch = [
        pltpu.make_async_copy(
            act.at[0, :, :, pl.ds(pl.multiple_of(zs[half + g] * TILE, 128), TILE)], acts.at[g], sems.at[g])
        for g in range(2)
    ]
    load = {}
    for n, pack in enumerate(("C", "AB")):
        span = pl.ds(COLUMNS[pack[0]][0], sum(COLUMNS[pack[-1]]) - COLUMNS[pack[0]][0])
        load[pack] = pltpu.make_async_copy(cot.at[0, :, :, span], cots.at[:, :, span], sems.at[2 + n])
    ask = pltpu.make_async_copy(order, asked, sems.at[4])
    ask.start()
    load["C"].start()
    fetch[0].start()
    ask.wait()
    alive = jnp.where(me == failed[0], 0, counts[0])
    live = [jnp.float32(0)] * SLOTS
    for position in range(SLOTS):
        for k in range(SLOTS):
            live[k] = jnp.where((asked[0, position] == k) & (position < alive), jnp.float32(1), live[k])
    if half == 2:
        alive_rows = jnp.full((8, COLUMNS["C"][1]), alive.astype(jnp.float32))
        outs[4][2 * TILE:, :] = alive_rows
        outs[5][...] = alive_rows
    for g in range(2):
        fetch[g].wait()
        rows = acts[g].reshape(K, TILE)
        for pack in ("C", "AB"):
            first, last = COLUMNS[pack[0]][0], sum(COLUMNS[pack[-1]])
            if g == 0:
                load[pack].wait()
                if pack == "C":
                    load["AB"].start()
                    fetch[1].start()
                for k in range(SLOTS):
                    cots[k, :, first:last] = cots[k, :, first:last] * live[k].astype(jnp.bfloat16)
            total[:, :last - first] = lax.dot_general(
                rows, cots[:, :, first:last].reshape(K, last - first), (((0,), (0,)), ((), ())),
                preferred_element_type=jnp.float32)
            for group in pack:
                column, columns = COLUMNS[group]
                for i in range(4):
                    for j in range(4):
                        start = (ys if group == "B" else xs)[group][i] * (160 if group == "B" else ROWS)
                        start += (xs if group == "B" else ys)[group][j] * (ROWS if group == "B" else 160)
                        block = total[pl.ds(pl.multiple_of(start, 8), ROWS), column - first:column - first + columns]
                        if group == "A":
                            outs[i // 2][i % 2, j, g] = block
                        elif group == "B":
                            outs[2 + i // 2][i % 2, g, j] = block
                        else:
                            outs[4][pl.ds(((g * 4 + i) * 4 + j) * ROWS, ROWS), :] = block


def partials(half, activations, cotangents, failed, counts, order):
    a, b, c = (COLUMNS[group][1] for group in "ABC")
    shapes = [(2, 4, 2, ROWS, a)] * 2 + [(2, 2, 4, ROWS, b)] * 2
    shapes += [(2 * TILE + 8, c), (8, c)] if half == 2 else [(2 * TILE, c)]
    return pl.pallas_call(
        functools.partial(products, half),
        out_shape=[jax.ShapeDtypeStruct(shape, jnp.float32) for shape in shapes],
        in_specs=[pl.BlockSpec(memory_space=pltpu.SMEM)] * 2 + [pl.BlockSpec(memory_space=pltpu.HBM)] * 3,
        out_specs=[pl.BlockSpec(memory_space=pltpu.VMEM)] * len(shapes),
        scratch_shapes=[
            pltpu.VMEM((2, SLOTS, TOKENS, TILE), jnp.bfloat16),
            pltpu.VMEM((SLOTS, TOKENS, a + b + c), jnp.bfloat16),
            pltpu.VMEM((TILE, max(a + b, c)), jnp.float32),
            pltpu.SMEM((1, SLOTS), jnp.int32),
            pltpu.SemaphoreType.DMA((5,)),
        ],
        compiler_params=pltpu.CompilerParams(vmem_limit_bytes=28 << 20),
        cost_estimate=pl.CostEstimate(flops=1024, bytes_accessed=1024, transcendentals=0),
    )(failed, counts, *(pltpu.with_memory_space_constraint(x, pltpu.HBM) for x in (order, activations, cotangents)))


def together(values):
    return list(lax.optimization_barrier(tuple(values)))


def shards(activations, cotangents, failed, counts, order):
    run = functools.partial(partials, failed=failed, counts=counts, order=order)
    *one, activations, cotangents = together([*run(2, activations, cotangents), activations, cotangents])
    a_keep_far, a_send_far, b_keep_far, b_send_far, c_send, c_total = one
    a_keep_near, a_send_near, b_keep_near, b_send_near, c_keep = run(0, activations, cotangents)
    taken = None

    def take(got):
        nonlocal taken
        taken = got if taken is None else together([got, taken])[0]
        return taken

    def both(keep, got, total, rows):
        total = total + got[2 * rows:]
        return jnp.concatenate([keep[rows:] + got[rows:2 * rows], total], axis=0), keep[:rows] + got[:rows], total

    a1f, b1f, c1 = exchange(a_send_far, "x", 0), exchange(b_send_far, "y", 0), exchange(c_send, "z", 0)
    a1n, b1n = exchange(a_send_near, "x", 0), exchange(b_send_near, "y", 0)
    a1f = take(a1f)
    a2f = exchange(a_keep_far[1] + a1f[1], "x", 1)
    b1f = take(b1f)
    b2f = exchange(b_keep_far[1] + b1f[1], "y", 1)
    c1 = take(c1)
    c_out, c_stay, c_total = both(c_keep, c1, c_total, TILE)
    c2 = exchange(c_out, "z", 1)
    a1n = take(a1n)
    a2n = exchange(a_keep_near[1] + a1n[1], "x", 1)
    b1n = take(b1n)
    b2n = exchange(b_keep_near[1] + b1n[1], "y", 1)
    a2f, b2f, c2, _ = together([a2f, b2f, c2, taken])
    taken = c2
    a_far = (a_keep_far[0] + a1f[0]) + a2f
    a3f = exchange(a_far[2:4], "y", 0, True)
    b_far = (b_keep_far[0] + b1f[0]) + b2f
    b3 = exchange(b_far, "z", 0)
    c_whole, c_total = c_stay + c2[:TILE], c_total + c2[TILE:]
    c3 = exchange(jnp.concatenate([c_whole[320:], c_total], axis=0), "x", 0, True)
    a2n = take(a2n)
    a_near = (a_keep_near[0] + a1n[0]) + a2n
    a3n = exchange(a_near[2:4], "y", 0, True)
    b2n = take(b2n)
    b_near = (b_keep_near[0] + b1n[0]) + b2n
    b3 = take(b3)
    b4 = exchange(b_near[1] + b3[1], "z", 1)
    c3 = take(c3)
    c_out, c_stay, c_total = both(c_whole[:320], c3, c_total, 160)
    c4 = exchange(c_out, "x", 1, True)
    a3f = take(a3f)
    a3n = take(a3n)
    a4 = exchange(jnp.concatenate([a_far[1] + a3f[1], a_near[1] + a3n[1]], axis=0), "y", 1, True)
    b4 = take(b4)
    b_whole = (b_near[0] + b3[0]) + b4
    b5 = exchange(b_whole[2:4], "x", 0, True)
    c4 = take(c4)
    c_whole, c_total = c_stay + c4[:160], c_total + c4[160:]
    c5 = exchange(jnp.concatenate([c_whole[80:], c_total], axis=0), "y", 0, True)
    a4 = take(a4)
    a_far, a_near = (a_far[0] + a3f[0]) + a4[:2], (a_near[0] + a3n[0]) + a4[2:]
    a5 = exchange(a_far, "z", 0)
    b5 = take(b5)
    b6 = exchange(b_whole[1] + b5[1], "x", 1, True)
    c5 = take(c5)
    c_out, c_stay, c_total = both(c_whole[:80], c5, c_total, 40)
    c6 = exchange(c_out, "y", 1, True)
    a5 = take(a5)
    a6 = exchange(a_near[1] + a5[1], "z", 1)
    b6, c6, a6 = together([b6, c6, a6])
    a = (a_near[0] + a5[0]) + a6
    b = (b_whole[0] + b5[0]) + b6
    c = c_stay + c6[:40]
    total = c_total + c6[40:]
    total = jnp.concatenate([total, total, total, total[:, :256]], axis=1)
    gradient = jnp.concatenate([a, b, c], axis=1)
    return (gradient.reshape(5, 8, 2560) / total).reshape(40, 2560)


def solution(mesh):
    in_specs = (
        P(("section", "dp"), None, None, None),
        P(("section", "dp"), None, None, None),
        P(),
        P("dp"),
        P("dp", None),
    )
    out_specs = P(("section", "dp"), None)
    return jax.shard_map(shards, mesh=mesh, in_specs=in_specs, out_specs=out_specs, check_vma=False)
```

```python
import functools

import jax
import jax.numpy as jnp
from jax import lax
from jax.experimental import pallas as pl
from jax.experimental.pallas import tpu as pltpu
from jax.sharding import PartitionSpec as P

SLOTS, TOKENS, ROWS = 6, 192, 40
K = SLOTS * TOKENS
TILE = 16 * ROWS
STRIDE = {"x": 1, "y": 4, "z": 16}
COLUMNS = {"A": (0, 896), "B": (896, 896), "C": (1792, 768)}


def exchange(value, axis, turn, other=False):
    pairs = []
    for section in range(2):
        flip, stride = 1 if (section == turn) != other else 3, STRIDE[axis]
        for d in range(64):
            p = d // stride % 4
            pairs.append((section * 64 + d, section * 64 + d + ((p ^ flip) - p) * stride))
    return lax.ppermute(value, ("section", "dp"), pairs)


def opposite(value, axis):
    stride = STRIDE[axis]
    places = [(d, d + ((d // stride % 4 ^ 2) - d // stride % 4) * stride) for d in range(64)]
    return lax.ppermute(value, "dp", places)


def products(half, failed, counts, order, act, cot, *refs):
    outs, (acts, cots, total, asked, sems) = refs[:-5], refs[-5:]
    section, me = lax.axis_index("section"), lax.axis_index("dp")
    flips = (0, 3 - 2 * section, 1 + 2 * section, 2)
    others = (0, 1 + 2 * section, 3 - 2 * section, 2)
    x, y, z = me % 4, me // 4 % 4, me // 16
    zs = [z ^ flip for flip in flips]
    xs = {group: [x ^ flip for flip in (flips if group == "A" else others)] for group in "ABC"}
    ys = {group: [y ^ flip for flip in (flips if group == "B" else others)] for group in "ABC"}
    fetch = [
        pltpu.make_async_copy(
            act.at[0, :, :, pl.ds(pl.multiple_of(zs[half + g] * TILE, 128), TILE)], acts.at[g], sems.at[g])
        for g in range(2)
    ]
    load = {}
    for n, pack in enumerate(("C", "AB")):
        span = pl.ds(COLUMNS[pack[0]][0], sum(COLUMNS[pack[-1]]) - COLUMNS[pack[0]][0])
        load[pack] = pltpu.make_async_copy(cot.at[0, :, :, span], cots.at[:, :, span], sems.at[2 + n])
    ask = pltpu.make_async_copy(order, asked, sems.at[4])
    ask.start()
    load["C"].start()
    fetch[0].start()
    ask.wait()
    alive = jnp.where(me == failed[0], 0, counts[0])
    live = [jnp.float32(0)] * SLOTS
    for position in range(SLOTS):
        for k in range(SLOTS):
            live[k] = jnp.where((asked[0, position] == k) & (position < alive), jnp.float32(1), live[k])
    if half == 2:
        alive_rows = jnp.full((8, COLUMNS["C"][1]), alive.astype(jnp.float32))
        outs[4][2 * TILE:, :] = alive_rows
        outs[5][...] = alive_rows
    for g in range(2):
        fetch[g].wait()
        rows = acts[g].reshape(K, TILE)
        for pack in ("C", "AB"):
            first, last = COLUMNS[pack[0]][0], sum(COLUMNS[pack[-1]])
            if g == 0:
                load[pack].wait()
                if pack == "C":
                    load["AB"].start()
                    fetch[1].start()
                for k in range(SLOTS):
                    cots[k, :, first:last] = cots[k, :, first:last] * live[k].astype(jnp.bfloat16)
            total[:, :last - first] = lax.dot_general(
                rows, cots[:, :, first:last].reshape(K, last - first), (((0,), (0,)), ((), ())),
                preferred_element_type=jnp.float32)
            for group in pack:
                column, columns = COLUMNS[group]
                for i in range(4):
                    for j in range(4):
                        start = (ys if group == "B" else xs)[group][i] * (160 if group == "B" else ROWS)
                        start += (xs if group == "B" else ys)[group][j] * (ROWS if group == "B" else 160)
                        block = total[pl.ds(pl.multiple_of(start, 8), ROWS), column - first:column - first + columns]
                        if group == "A":
                            outs[i // 2][i % 2, j, g] = block
                        elif group == "B":
                            outs[2 + i // 2][i % 2, g, j] = block
                        else:
                            outs[4][pl.ds(((g * 4 + i) * 4 + j) * ROWS, ROWS), :] = block


def partials(half, activations, cotangents, failed, counts, order):
    a, b, c = (COLUMNS[group][1] for group in "ABC")
    shapes = [(2, 4, 2, ROWS, a)] * 2 + [(2, 2, 4, ROWS, b)] * 2
    shapes += [(2 * TILE + 8, c), (8, c)] if half == 2 else [(2 * TILE, c)]
    return pl.pallas_call(
        functools.partial(products, half),
        out_shape=[jax.ShapeDtypeStruct(shape, jnp.float32) for shape in shapes],
        in_specs=[pl.BlockSpec(memory_space=pltpu.SMEM)] * 2 + [pl.BlockSpec(memory_space=pltpu.HBM)] * 3,
        out_specs=[pl.BlockSpec(memory_space=pltpu.VMEM)] * len(shapes),
        scratch_shapes=[
            pltpu.VMEM((2, SLOTS, TOKENS, TILE), jnp.bfloat16),
            pltpu.VMEM((SLOTS, TOKENS, a + b + c), jnp.bfloat16),
            pltpu.VMEM((TILE, max(a + b, c)), jnp.float32),
            pltpu.SMEM((1, SLOTS), jnp.int32),
            pltpu.SemaphoreType.DMA((5,)),
        ],
        compiler_params=pltpu.CompilerParams(vmem_limit_bytes=28 << 20),
        cost_estimate=pl.CostEstimate(flops=1024, bytes_accessed=1024, transcendentals=0),
    )(failed, counts, *(pltpu.with_memory_space_constraint(x, pltpu.HBM) for x in (order, activations, cotangents)))


def together(values):
    return list(lax.optimization_barrier(tuple(values)))


def shards(activations, cotangents, failed, counts, order):
    run = functools.partial(partials, failed=failed, counts=counts, order=order)
    *one, activations, cotangents = together([*run(2, activations, cotangents), activations, cotangents])
    a_keep_far, a_send_far, b_keep_far, b_send_far, c_send, c_total = one
    a_keep_near, a_send_near, b_keep_near, b_send_near, c_keep = run(0, activations, cotangents)
    taken = None

    def take(got):
        nonlocal taken
        taken = got if taken is None else together([got, taken])[0]
        return taken

    def both(keep, got, total, rows):
        total = total + got[2 * rows:]
        return jnp.concatenate([keep[rows:] + got[rows:2 * rows], total], axis=0), keep[:rows] + got[:rows], total

    a1f, b1f, c1 = exchange(a_send_far, "x", 0), exchange(b_send_far, "y", 0), exchange(c_send, "z", 0)
    a1n, b1n = exchange(a_send_near, "x", 0), exchange(b_send_near, "y", 0)
    a1f = take(a1f)
    a2f = exchange(a_keep_far[1] + a1f[1], "x", 1)
    b1f = take(b1f)
    b2f = exchange(b_keep_far[1] + b1f[1], "y", 1)
    c1 = take(c1)
    c_out, c_stay, c_total = both(c_keep, c1, c_total, TILE)
    c2 = exchange(c_out, "z", 1)
    a1n = take(a1n)
    a2n = exchange(a_keep_near[1] + a1n[1], "x", 1)
    b1n = take(b1n)
    b2n = exchange(b_keep_near[1] + b1n[1], "y", 1)
    a2f, b2f, c2, _ = together([a2f, b2f, c2, taken])
    taken = c2
    a_far = (a_keep_far[0] + a1f[0]) + a2f
    a3f = exchange(a_far[2:4], "y", 0, True)
    b_far = (b_keep_far[0] + b1f[0]) + b2f
    b3 = exchange(b_far, "z", 0)
    c_whole, c_total = c_stay + c2[:TILE], c_total + c2[TILE:]
    c3 = exchange(jnp.concatenate([c_whole[320:], c_total], axis=0), "x", 0, True)
    a2n = take(a2n)
    a_near = (a_keep_near[0] + a1n[0]) + a2n
    a3n = exchange(a_near[2:4], "y", 0, True)
    b2n = take(b2n)
    b_near = (b_keep_near[0] + b1n[0]) + b2n
    b3 = take(b3)
    b4 = exchange(b_near[1] + b3[1], "z", 1)
    c3 = take(c3)
    c_out, c_stay, c_total = both(c_whole[:320], c3, c_total, 160)
    c4 = exchange(c_out, "x", 1, True)
    a3f = take(a3f)
    a3n = take(a3n)
    a4 = exchange(jnp.concatenate([a_far[1] + a3f[1], a_near[1] + a3n[1]], axis=0), "y", 1, True)
    b4 = take(b4)
    b_whole = (b_near[0] + b3[0]) + b4
    b5 = [exchange(b_whole[2], "x", 0, True), exchange(b_whole[1], "x", 1, True), opposite(b_whole[3], "x")]
    c4 = take(c4)
    c_whole, c_total = c_stay + c4[:160], c_total + c4[160:]
    outs = [jnp.concatenate([c_whole[40 * k:40 * (k + 1)], c_total], axis=0) for k in range(4)]
    c5 = [exchange(outs[2], "y", 0, True), exchange(outs[1], "y", 1, True), opposite(outs[3], "y")]
    a4 = together([a4, b5[0], taken])[0]
    a_far, a_near = (a_far[0] + a3f[0]) + a4[:2], (a_near[0] + a3n[0]) + a4[2:]
    a5 = [exchange(a_far[0], "z", 0), exchange(a_near[1], "z", 1), opposite(a_far[1], "z")]
    *b5, taken = together([*b5, taken])
    *c5, taken = together([*c5, b5[2]])
    *a5, taken = together([*a5, c5[2]])
    a = ((a_near[0] + a5[0]) + a5[1]) + a5[2]
    b = ((b_whole[0] + b5[0]) + b5[1]) + b5[2]
    c = ((outs[0] + c5[0]) + c5[1]) + c5[2]
    total = c[40:]
    c = c[:40]
    total = jnp.concatenate([total, total, total, total[:, :256]], axis=1)
    gradient = jnp.concatenate([a, b, c], axis=1)
    return (gradient.reshape(5, 8, 2560) / total).reshape(40, 2560)


def solution(mesh):
    in_specs = (
        P(("section", "dp"), None, None, None),
        P(("section", "dp"), None, None, None),
        P(),
        P("dp"),
        P("dp", None),
    )
    out_specs = P(("section", "dp"), None)
    return jax.shard_map(shards, mesh=mesh, in_specs=in_specs, out_specs=out_specs, check_vma=False)
```

```python
import functools

import jax
import jax.numpy as jnp
from jax import lax
from jax.experimental import pallas as pl
from jax.experimental.pallas import tpu as pltpu
from jax.sharding import PartitionSpec as P

SLOTS, TOKENS, ROWS = 6, 192, 40
K = SLOTS * TOKENS
TILE = 16 * ROWS
STRIDE = {"x": 1, "y": 4, "z": 16}
COLUMNS = {"A": (0, 896), "B": (896, 896), "C": (1792, 768)}


def exchange(value, axis, turn, other=False):
    pairs = []
    for section in range(2):
        flip, stride = 1 if (section == turn) != other else 3, STRIDE[axis]
        for d in range(64):
            p = d // stride % 4
            pairs.append((section * 64 + d, section * 64 + d + ((p ^ flip) - p) * stride))
    return lax.ppermute(value, ("section", "dp"), pairs)


def opposite(value, axis):
    stride = STRIDE[axis]
    places = [(d, d + ((d // stride % 4 ^ 2) - d // stride % 4) * stride) for d in range(64)]
    return lax.ppermute(value, "dp", places)


def products(half, failed, counts, order, act, cot, *refs):
    outs, (acts, cots, total, asked, sems) = refs[:-5], refs[-5:]
    section, me = lax.axis_index("section"), lax.axis_index("dp")
    flips = (0, 3 - 2 * section, 1 + 2 * section, 2)
    others = (0, 1 + 2 * section, 3 - 2 * section, 2)
    x, y, z = me % 4, me // 4 % 4, me // 16
    zs = [z ^ flip for flip in flips]
    xs = {group: [x ^ flip for flip in (flips if group == "A" else others)] for group in "ABC"}
    ys = {group: [y ^ flip for flip in (flips if group == "B" else others)] for group in "ABC"}
    fetch = [
        pltpu.make_async_copy(
            act.at[0, :, :, pl.ds(pl.multiple_of(zs[half + g] * TILE, 128), TILE)],
            acts.at[:, :, pl.ds(g * TILE, TILE)], sems.at[g])
        for g in range(2)
    ]
    load = {}
    for n, pack in enumerate(("C", "AB")):
        span = pl.ds(COLUMNS[pack[0]][0], sum(COLUMNS[pack[-1]]) - COLUMNS[pack[0]][0])
        load[pack] = pltpu.make_async_copy(cot.at[0, :, :, span], cots.at[:, :, span], sems.at[2 + n])
    ask = pltpu.make_async_copy(order, asked, sems.at[4])
    ask.start()
    load["C"].start()
    fetch[0].start()
    if half == 2:
        fetch[1].start()
    ask.wait()
    alive = jnp.where(me == failed[0], 0, counts[0])
    live = [jnp.float32(0)] * SLOTS
    for position in range(SLOTS):
        for k in range(SLOTS):
            live[k] = jnp.where((asked[0, position] == k) & (position < alive), jnp.float32(1), live[k])
    if half == 2:
        alive_rows = jnp.full((8, COLUMNS["C"][1]), alive.astype(jnp.float32))
        outs[4][2 * TILE:, :] = alive_rows
        outs[5][...] = alive_rows
    tiles = 2 if half == 2 else 1
    for step in range(2 // tiles):
        for g in range(step * tiles, step * tiles + tiles):
            fetch[g].wait()
        rows = acts[:, :, step * TILE:(step + tiles) * TILE].reshape(K, tiles * TILE)
        for pack in ("C", "AB"):
            first, last = COLUMNS[pack[0]][0], sum(COLUMNS[pack[-1]])
            if step == 0:
                load[pack].wait()
                if pack == "C":
                    load["AB"].start()
                    if tiles == 1:
                        fetch[1].start()
                for k in range(SLOTS):
                    cots[k, :, first:last] = cots[k, :, first:last] * live[k].astype(jnp.bfloat16)
            total[:, :last - first] = lax.dot_general(
                rows, cots[:, :, first:last].reshape(K, last - first), (((0,), (0,)), ((), ())),
                preferred_element_type=jnp.float32)
            for g in range(step * tiles, step * tiles + tiles):
                for group in pack:
                    column, columns = COLUMNS[group]
                    for i in range(4):
                        for j in range(4):
                            start = (ys if group == "B" else xs)[group][i] * (160 if group == "B" else ROWS)
                            start += (xs if group == "B" else ys)[group][j] * (ROWS if group == "B" else 160)
                            start += g % tiles * TILE
                            block = total[pl.ds(pl.multiple_of(start, 8), ROWS), column - first:column - first + columns]
                            if group == "A":
                                outs[i // 2][i % 2, j, g] = block
                            elif group == "B":
                                outs[2 + i // 2][i % 2, g, j] = block
                            else:
                                outs[4][pl.ds(((g * 4 + i) * 4 + j) * ROWS, ROWS), :] = block


def partials(half, activations, cotangents, failed, counts, order):
    a, b, c = (COLUMNS[group][1] for group in "ABC")
    shapes = [(2, 4, 2, ROWS, a)] * 2 + [(2, 2, 4, ROWS, b)] * 2
    shapes += [(2 * TILE + 8, c), (8, c)] if half == 2 else [(2 * TILE, c)]
    return pl.pallas_call(
        functools.partial(products, half),
        out_shape=[jax.ShapeDtypeStruct(shape, jnp.float32) for shape in shapes],
        in_specs=[pl.BlockSpec(memory_space=pltpu.SMEM)] * 2 + [pl.BlockSpec(memory_space=pltpu.HBM)] * 3,
        out_specs=[pl.BlockSpec(memory_space=pltpu.VMEM)] * len(shapes),
        scratch_shapes=[
            pltpu.VMEM((SLOTS, TOKENS, 2 * TILE), jnp.bfloat16),
            pltpu.VMEM((SLOTS, TOKENS, a + b + c), jnp.bfloat16),
            pltpu.VMEM((TILE * (2 if half == 2 else 1), max(a + b, c)), jnp.float32),
            pltpu.SMEM((1, SLOTS), jnp.int32),
            pltpu.SemaphoreType.DMA((5,)),
        ],
        compiler_params=pltpu.CompilerParams(vmem_limit_bytes=(33 if half == 2 else 28) << 20),
        cost_estimate=pl.CostEstimate(flops=1024, bytes_accessed=1024, transcendentals=0),
    )(failed, counts, *(pltpu.with_memory_space_constraint(x, pltpu.HBM) for x in (order, activations, cotangents)))


def together(values):
    return list(lax.optimization_barrier(tuple(values)))


def shards(activations, cotangents, failed, counts, order):
    run = functools.partial(partials, failed=failed, counts=counts, order=order)
    *one, activations, cotangents = together([*run(2, activations, cotangents), activations, cotangents])
    a_keep_far, a_send_far, b_keep_far, b_send_far, c_send, c_total = one
    a_keep_near, a_send_near, b_keep_near, b_send_near, c_keep = run(0, activations, cotangents)
    taken = None

    def take(got):
        nonlocal taken
        taken = got if taken is None else together([got, taken])[0]
        return taken

    def both(keep, got, total, rows):
        total = total + got[2 * rows:]
        return jnp.concatenate([keep[rows:] + got[rows:2 * rows], total], axis=0), keep[:rows] + got[:rows], total

    a1f, b1f, c1 = exchange(a_send_far, "x", 0), exchange(b_send_far, "y", 0), exchange(c_send, "z", 0)
    a1n, b1n = exchange(a_send_near, "x", 0), exchange(b_send_near, "y", 0)
    a1f = take(a1f)
    a2f = exchange(a_keep_far[1] + a1f[1], "x", 1)
    b1f = take(b1f)
    b2f = exchange(b_keep_far[1] + b1f[1], "y", 1)
    c1 = take(c1)
    c_out, c_stay, c_total = both(c_keep, c1, c_total, TILE)
    c2 = exchange(c_out, "z", 1)
    a1n = take(a1n)
    a2n = exchange(a_keep_near[1] + a1n[1], "x", 1)
    b1n = take(b1n)
    b2n = exchange(b_keep_near[1] + b1n[1], "y", 1)
    a2f, b2f, c2, _ = together([a2f, b2f, c2, taken])
    taken = c2
    a_far = (a_keep_far[0] + a1f[0]) + a2f
    a3f = exchange(a_far[2:4], "y", 0, True)
    b_far = (b_keep_far[0] + b1f[0]) + b2f
    b3 = exchange(b_far, "z", 0)
    c_whole, c_total = c_stay + c2[:TILE], c_total + c2[TILE:]
    c3 = exchange(jnp.concatenate([c_whole[320:], c_total], axis=0), "x", 0, True)
    a2n = take(a2n)
    a_near = (a_keep_near[0] + a1n[0]) + a2n
    a3n = exchange(a_near[2:4], "y", 0, True)
    b2n = take(b2n)
    b_near = (b_keep_near[0] + b1n[0]) + b2n
    b3 = take(b3)
    b4 = exchange(b_near[1] + b3[1], "z", 1)
    c3 = take(c3)
    c_out, c_stay, c_total = both(c_whole[:320], c3, c_total, 160)
    c4 = exchange(c_out, "x", 1, True)
    a3f = take(a3f)
    a3n = take(a3n)
    a4 = exchange(jnp.concatenate([a_far[1] + a3f[1], a_near[1] + a3n[1]], axis=0), "y", 1, True)
    b4 = take(b4)
    b_whole = (b_near[0] + b3[0]) + b4
    b5 = exchange(b_whole[2:4], "x", 0, True)
    c4 = take(c4)
    c_whole, c_total = c_stay + c4[:160], c_total + c4[160:]
    c5 = exchange(jnp.concatenate([c_whole[80:], c_total], axis=0), "y", 0, True)
    a4 = take(a4)
    a_far, a_near = (a_far[0] + a3f[0]) + a4[:2], (a_near[0] + a3n[0]) + a4[2:]
    a5 = [exchange(a_far[0], "z", 0), exchange(a_near[1], "z", 1), opposite(a_far[1], "z")]
    b5 = take(b5)
    b6 = exchange(b_whole[1] + b5[1], "x", 1, True)
    c5 = take(c5)
    c_out, c_stay, c_total = both(c_whole[:80], c5, c_total, 40)
    c6 = exchange(c_out, "y", 1, True)
    b6, c6, *a5 = together([b6, c6, *a5])
    a = ((a_near[0] + a5[0]) + a5[1]) + a5[2]
    b = (b_whole[0] + b5[0]) + b6
    c = c_stay + c6[:40]
    total = c_total + c6[40:]
    total = jnp.concatenate([total, total, total, total[:, :256]], axis=1)
    gradient = jnp.concatenate([a, b, c], axis=1)
    return (gradient.reshape(5, 8, 2560) / total).reshape(40, 2560)


def solution(mesh):
    in_specs = (
        P(("section", "dp"), None, None, None),
        P(("section", "dp"), None, None, None),
        P(),
        P("dp"),
        P("dp", None),
    )
    out_specs = P(("section", "dp"), None)
    return jax.shard_map(shards, mesh=mesh, in_specs=in_specs, out_specs=out_specs, check_vma=False)
```

```python
import functools

import jax
import jax.numpy as jnp
from jax import lax
from jax.experimental import pallas as pl
from jax.experimental.pallas import tpu as pltpu
from jax.sharding import PartitionSpec as P

SLOTS, TOKENS, ROWS = 6, 192, 40
K = SLOTS * TOKENS
TILE = 16 * ROWS
STRIDE = {"x": 1, "y": 4, "z": 16}
COLUMNS = {"A": (0, 896), "B": (896, 896), "C": (1792, 768)}


def exchange(value, axis, turn, other=False):
    pairs = []
    for section in range(2):
        flip, stride = 1 if (section == turn) == other else 3, STRIDE[axis]
        for d in range(64):
            p = d // stride % 4
            pairs.append((section * 64 + d, section * 64 + d + ((p ^ flip) - p) * stride))
    return lax.ppermute(value, ("section", "dp"), pairs)


def products(half, failed, counts, order, act, cot, *refs):
    outs, (acts, cots, total, asked, sems) = refs[:-5], refs[-5:]
    section, me = lax.axis_index("section"), lax.axis_index("dp")
    flips = (0, 1 + 2 * section, 3 - 2 * section, 2)
    others = (0, 3 - 2 * section, 1 + 2 * section, 2)
    x, y, z = me % 4, me // 4 % 4, me // 16
    zs = [z ^ flip for flip in flips]
    xs = {group: [x ^ flip for flip in (flips if group == "A" else others)] for group in "ABC"}
    ys = {group: [y ^ flip for flip in (flips if group == "B" else others)] for group in "ABC"}
    fetch = [
        pltpu.make_async_copy(
            act.at[0, :, :, pl.ds(pl.multiple_of(zs[half + g] * TILE, 128), TILE)], acts.at[g], sems.at[g])
        for g in range(2)
    ]
    load = {}
    for n, pack in enumerate(("C", "AB")):
        span = pl.ds(COLUMNS[pack[0]][0], sum(COLUMNS[pack[-1]]) - COLUMNS[pack[0]][0])
        load[pack] = pltpu.make_async_copy(cot.at[0, :, :, span], cots.at[:, :, span], sems.at[2 + n])
    ask = pltpu.make_async_copy(order, asked, sems.at[4])
    ask.start()
    load["C"].start()
    fetch[0].start()
    ask.wait()
    alive = jnp.where(me == failed[0], 0, counts[0])
    live = [jnp.float32(0)] * SLOTS
    for position in range(SLOTS):
        for k in range(SLOTS):
            live[k] = jnp.where((asked[0, position] == k) & (position < alive), jnp.float32(1), live[k])
    if half == 2:
        alive_rows = jnp.full((8, COLUMNS["C"][1]), alive.astype(jnp.float32))
        outs[4][2 * TILE:, :] = alive_rows
        outs[5][...] = alive_rows
    for g in range(2):
        fetch[g].wait()
        rows = acts[g].reshape(K, TILE)
        for pack in ("C", "AB"):
            first, last = COLUMNS[pack[0]][0], sum(COLUMNS[pack[-1]])
            if g == 0:
                load[pack].wait()
                if pack == "C":
                    load["AB"].start()
                    fetch[1].start()
                for k in range(SLOTS):
                    cots[k, :, first:last] = cots[k, :, first:last] * live[k].astype(jnp.bfloat16)
            total[:, :last - first] = lax.dot_general(
                rows, cots[:, :, first:last].reshape(K, last - first), (((0,), (0,)), ((), ())),
                preferred_element_type=jnp.float32)
            for group in pack:
                column, columns = COLUMNS[group]
                for i in range(4):
                    for j in range(4):
                        start = (ys if group == "B" else xs)[group][i] * (160 if group == "B" else ROWS)
                        start += (xs if group == "B" else ys)[group][j] * (ROWS if group == "B" else 160)
                        block = total[pl.ds(pl.multiple_of(start, 8), ROWS), column - first:column - first + columns]
                        if group == "A":
                            outs[i // 2][i % 2, j, g] = block
                        elif group == "B":
                            outs[2 + i // 2][i % 2, g, j] = block
                        else:
                            outs[4][pl.ds(((g * 4 + i) * 4 + j) * ROWS, ROWS), :] = block


def partials(half, activations, cotangents, failed, counts, order):
    a, b, c = (COLUMNS[group][1] for group in "ABC")
    shapes = [(2, 4, 2, ROWS, a)] * 2 + [(2, 2, 4, ROWS, b)] * 2
    shapes += [(2 * TILE + 8, c), (8, c)] if half == 2 else [(2 * TILE, c)]
    return pl.pallas_call(
        functools.partial(products, half),
        out_shape=[jax.ShapeDtypeStruct(shape, jnp.float32) for shape in shapes],
        in_specs=[pl.BlockSpec(memory_space=pltpu.SMEM)] * 2 + [pl.BlockSpec(memory_space=pltpu.HBM)] * 3,
        out_specs=[pl.BlockSpec(memory_space=pltpu.VMEM)] * len(shapes),
        scratch_shapes=[
            pltpu.VMEM((2, SLOTS, TOKENS, TILE), jnp.bfloat16),
            pltpu.VMEM((SLOTS, TOKENS, a + b + c), jnp.bfloat16),
            pltpu.VMEM((TILE, max(a + b, c)), jnp.float32),
            pltpu.SMEM((1, SLOTS), jnp.int32),
            pltpu.SemaphoreType.DMA((5,)),
        ],
        compiler_params=pltpu.CompilerParams(vmem_limit_bytes=28 << 20),
        cost_estimate=pl.CostEstimate(flops=1024, bytes_accessed=1024, transcendentals=0),
    )(failed, counts, *(pltpu.with_memory_space_constraint(x, pltpu.HBM) for x in (order, activations, cotangents)))


def together(values):
    return list(lax.optimization_barrier(tuple(values)))


def shards(activations, cotangents, failed, counts, order):
    run = functools.partial(partials, failed=failed, counts=counts, order=order)
    *one, activations, cotangents = together([*run(2, activations, cotangents), activations, cotangents])
    a_keep_far, a_send_far, b_keep_far, b_send_far, c_send, c_total = one
    a_keep_near, a_send_near, b_keep_near, b_send_near, c_keep = run(0, activations, cotangents)
    taken = None

    def take(got):
        nonlocal taken
        taken = got if taken is None else together([got, taken])[0]
        return taken

    def both(keep, got, total, rows):
        total = total + got[2 * rows:]
        return jnp.concatenate([keep[rows:] + got[rows:2 * rows], total], axis=0), keep[:rows] + got[:rows], total

    a1f, b1f, c1 = exchange(a_send_far, "x", 0), exchange(b_send_far, "y", 0), exchange(c_send, "z", 0)
    a1n, b1n = exchange(a_send_near, "x", 0), exchange(b_send_near, "y", 0)
    a1f = take(a1f)
    a2f = exchange(a_keep_far[1] + a1f[1], "x", 1)
    b1f = take(b1f)
    b2f = exchange(b_keep_far[1] + b1f[1], "y", 1)
    c1 = take(c1)
    c_out, c_stay, c_total = both(c_keep, c1, c_total, TILE)
    c2 = exchange(c_out, "z", 1)
    a1n = take(a1n)
    a2n = exchange(a_keep_near[1] + a1n[1], "x", 1)
    b1n = take(b1n)
    b2n = exchange(b_keep_near[1] + b1n[1], "y", 1)
    a2f, b2f, c2, _ = together([a2f, b2f, c2, taken])
    taken = c2
    a_far = (a_keep_far[0] + a1f[0]) + a2f
    a3f = exchange(a_far[2:4], "y", 0, True)
    b_far = (b_keep_far[0] + b1f[0]) + b2f
    b3 = exchange(b_far, "z", 0)
    c_whole, c_total = c_stay + c2[:TILE], c_total + c2[TILE:]
    c3 = exchange(jnp.concatenate([c_whole[320:], c_total], axis=0), "x", 0, True)
    a2n = take(a2n)
    a_near = (a_keep_near[0] + a1n[0]) + a2n
    a3n = exchange(a_near[2:4], "y", 0, True)
    b2n = take(b2n)
    b_near = (b_keep_near[0] + b1n[0]) + b2n
    b3 = take(b3)
    b4 = exchange(b_near[1] + b3[1], "z", 1)
    c3 = take(c3)
    c_out, c_stay, c_total = both(c_whole[:320], c3, c_total, 160)
    c4 = exchange(c_out, "x", 1, True)
    a3f = take(a3f)
    a3n = take(a3n)
    a4 = exchange(jnp.concatenate([a_far[1] + a3f[1], a_near[1] + a3n[1]], axis=0), "y", 1, True)
    b4 = take(b4)
    b_whole = (b_near[0] + b3[0]) + b4
    b5 = exchange(b_whole[2:4], "x", 0, True)
    c4 = take(c4)
    c_whole, c_total = c_stay + c4[:160], c_total + c4[160:]
    c5 = exchange(jnp.concatenate([c_whole[80:], c_total], axis=0), "y", 0, True)
    a4 = take(a4)
    a_far, a_near = (a_far[0] + a3f[0]) + a4[:2], (a_near[0] + a3n[0]) + a4[2:]
    a5 = exchange(a_far, "z", 0)
    b5 = take(b5)
    b6 = exchange(b_whole[1] + b5[1], "x", 1, True)
    c5 = take(c5)
    c_out, c_stay, c_total = both(c_whole[:80], c5, c_total, 40)
    c6 = exchange(c_out, "y", 1, True)
    a5 = take(a5)
    a6 = exchange(a_near[1] + a5[1], "z", 1)
    b6, c6, a6 = together([b6, c6, a6])
    a = (a_near[0] + a5[0]) + a6
    b = (b_whole[0] + b5[0]) + b6
    c = c_stay + c6[:40]
    total = c_total + c6[40:]
    total = jnp.concatenate([total, total, total, total[:, :256]], axis=1)
    gradient = jnp.concatenate([a, b, c], axis=1)
    return (gradient.reshape(5, 8, 2560) / total).reshape(40, 2560)


def solution(mesh):
    in_specs = (
        P(("section", "dp"), None, None, None),
        P(("section", "dp"), None, None, None),
        P(),
        P("dp"),
        P("dp", None),
    )
    out_specs = P(("section", "dp"), None)
    return jax.shard_map(shards, mesh=mesh, in_specs=in_specs, out_specs=out_specs, check_vma=False)
```
